32 devices in a mesh: ind: 16 (over z, y, x), snp: 2 (over core).
Axes of the slice: x: 2, y: 2, z: 4, core: 2. Of those that a mesh axis runs over, the one named last changes fastest.
Arguments:
- genotypes: int32 [1024, 4096], P('ind', 'snp'), may hold values from 0 to 2
- observed: int32 [1024, 4096], P('ind', 'snp'), may hold values from 0 to 1
- ancestry: float32 [1024, 32], P('ind'), may hold values from 0.018 to 54.6, as said below
- freqs: float32 [4096, 32], P(('snp', 'ind')), may hold values from 0.05 to 0.95
Outputs:
- ancestry_out: float32 [1024, 32], P('ind')
- freqs_out: float32 [4096, 32], P(('snp', 'ind'))
The draws below stay inside these ranges and needn't reach their ends.
Inputs may be any that keep to these rules, and one draw needn't show every extreme that they name: `ancestry`: positive weights.
All inputs are finite; a program needn't handle non-finite values.
Results may differ from the reference program's by a relative error of at most 0.0003.
Values sent between devices are 32-bit elements; how exact they have to be, the bound alone decides.
A program may use at most 64 MiB of HBM per device.

```python
import jax
import jax.numpy as jnp
from jax import lax

K = 32
ND = 64
STEPS = 3
N = 1024
M = 4096


def draw_observed(key, part):
    rows = jnp.arange(N, dtype=jnp.int32)[:, None]
    rate = 30 + 65 * rows // (N - 1)
    roll = jax.random.randint(jax.random.fold_in(key, 11), (N, M), 0, 100, dtype=jnp.int32)
    return (roll < rate).astype(jnp.int32)


def draw_ancestry(key, part):
    spread = 0.5 + 3.5 * jnp.arange(N, dtype=jnp.float32)[:, None] / (N - 1)
    inner = jax.random.fold_in(key, 23)
    unit = jnp.clip(0.5 * jax.random.normal(inner, (N, K), jnp.float32), -1.0, 1.0)
    return jnp.exp(unit * spread).astype(jnp.float32)


def set_ends(array, key, smallest, top_value):
    extent = array.shape
    spot = [jax.random.randint(jax.random.fold_in(key, axis), (), 0, extent[axis]) for axis in range(len(extent))]
    array = array.at[tuple(spot)].set(smallest)
    longest = extent.index(max(extent))
    spot[longest] = (spot[longest] + 1) % extent[longest]
    return array.at[tuple(spot)].set(top_value)


def level_of(rng, extent, shards, smallest, high):
    def one(position, parts):
        heights = jax.random.uniform(jax.random.fold_in(jax.random.fold_in(rng, 6), position), (parts,), jnp.float32, smallest / len(shards), high / len(shards))
        return jnp.repeat(jnp.exp(heights), extent[position] // parts).reshape((-1,) + (1,) * (len(extent) - position - 1))

    level = one(*shards[0])
    for cut in shards[1:]:
        level = level * one(*cut)
    return level


def setup_inputs(seed: int = 0) -> dict:
    keys = jax.random.split(jax.random.key(seed), 5)
    return {
        "genotypes": set_ends(jax.random.randint(keys[0], (N, M), 0, 3), jax.random.fold_in(keys[0], 1), 0, 2).astype(jnp.int32),
        "observed": draw_observed(jax.random.fold_in(keys[4], 71), 0),
        "ancestry": draw_ancestry(jax.random.fold_in(keys[4], 71), 0),
        "freqs": jnp.clip(0.05 + 0.9 * jax.random.uniform(keys[3], (M, K), jnp.float32) ** level_of(keys[3], (M, K), ((0, 32),), -0.2, 0.2), 0.05, 0.95),
    }


clip_low = 1e-05
high = lax.Precision.HIGHEST

def em_map(hits, misses, q, f):
    blocks = q.shape[0] // ND
    width = f.shape[0]
    hit_blocks = hits.reshape(blocks, ND, width)
    miss_blocks = misses.reshape(blocks, ND, width)
    q_blocks = q.reshape(blocks, ND, q.shape[1])

    def one_block(carry, items):
        hit_rows, miss_rows, q_rows = items
        prob = jnp.dot(q_rows, f.T, precision=high, preferred_element_type=jnp.float32)
        ratio_a = hit_rows / prob
        ratio_b = miss_rows / (1.0 - prob)
        sum_a = jnp.dot(ratio_a, f, precision=high, preferred_element_type=jnp.float32)
        sum_b = jnp.dot(ratio_b, 1.0 - f, precision=high, preferred_element_type=jnp.float32)
        q_next = q_rows * (sum_a + sum_b)
        q_next = q_next / lax.optimization_barrier(jnp.sum(q_next, axis=1, keepdims=True))
        c_part = jnp.dot(ratio_a.T, q_rows, precision=high, preferred_element_type=jnp.float32)
        d_part = jnp.dot(ratio_b.T, q_rows, precision=high, preferred_element_type=jnp.float32)
        return ((carry[0] + c_part, carry[1] + d_part), q_next)
    start = (jnp.zeros(f.shape, jnp.float32), jnp.zeros(f.shape, jnp.float32))
    (c_total, d_total), q_new = lax.scan(one_block, start, (hit_blocks, miss_blocks, q_blocks))
    f_new = f * c_total / (f * c_total + (1.0 - f) * d_total)
    return (q_new.reshape(q.shape), f_new)

def reference(genotypes, observed, ancestry, freqs):
    geno = genotypes.astype(jnp.float32)
    seen = observed.astype(jnp.float32)
    hits = seen * geno
    misses = seen * (2.0 - geno)
    q_zero = ancestry / lax.optimization_barrier(jnp.sum(ancestry, axis=1, keepdims=True))
    f_zero = freqs
    for step in range(STEPS):
        q_one, f_one = em_map(hits, misses, q_zero, f_zero)
        q_two, f_two = em_map(hits, misses, q_one, f_one)
        rq = q_one - q_zero
        rf = f_one - f_zero
        vq = q_two - 2.0 * q_one + q_zero
        vf = f_two - 2.0 * f_one + f_zero
        first = jnp.sum(rq * rq) + jnp.sum(rf * rf)
        second = jnp.sum(vq * vq) + jnp.sum(vf * vf)
        alpha = -jnp.sqrt(first / (second + 1e-20))
        q_ext = jnp.clip(q_zero - 2.0 * alpha * rq + alpha * alpha * vq, clip_low, 1.0 - clip_low)
        q_zero = q_ext / lax.optimization_barrier(jnp.sum(q_ext, axis=1, keepdims=True))
        f_zero = jnp.clip(f_zero - 2.0 * alpha * rf + alpha * alpha * vf, clip_low, 1.0 - clip_low)
    return (q_zero, f_zero)
```

```python
import functools

import jax
import jax.numpy as jnp
from jax import lax
from jax.experimental import pallas as pl
from jax.experimental.pallas import tpu as pltpu
from jax.sharding import PartitionSpec as P

STEPS = 3


clip_low = 1e-05
high = lax.Precision.HIGHEST
MESH = pl.DeviceIdType.MESH
f32 = jnp.float32
bf16 = jnp.bfloat16


def over_rows(left, right):
    return lax.dot_general(
        left, right, (((0,), (0,)), ((), ())), precision=high, preferred_element_type=jnp.float32
    )


def per_device(genotypes, observed, ancestry, freqs):
    ind_count = lax.axis_size("ind")
    snp_count = lax.axis_size("snp")
    geno = genotypes.astype(jnp.float32)
    seen = observed.astype(jnp.float32)
    hits = seen * geno
    misses = seen * (2.0 - geno)
    own_rows = freqs.shape[0]
    q_zero = ancestry / jnp.sum(ancestry, axis=1, keepdims=True)
    f_zero = lax.all_gather(freqs, "ind", axis=0, tiled=True)
    f_weight = 1.0 / ind_count
    q_weight = 1.0 / snp_count

    def em_map(q_rows, f_state):
        prob = jnp.dot(q_rows, f_state.T, precision=high, preferred_element_type=jnp.float32)
        ratio_a = hits / prob
        ratio_b = misses / (1.0 - prob)
        sum_a = jnp.dot(ratio_a, f_state, precision=high, preferred_element_type=jnp.float32)
        sum_b = jnp.dot(ratio_b, 1.0 - f_state, precision=high, preferred_element_type=jnp.float32)
        c_part = over_rows(ratio_a, q_rows)
        d_part = over_rows(ratio_b, q_rows)
        sum_a, sum_b = lax.psum((sum_a, sum_b), "snp")
        q_next = q_rows * (sum_a + sum_b)
        q_next = q_next / jnp.sum(q_next, axis=1, keepdims=True)
        c_total, d_total = lax.psum((c_part, d_part), "ind")
        f_next = f_state * c_total / (f_state * c_total + (1.0 - f_state) * d_total)
        return (q_next, f_next)

    for step in range(STEPS):
        q_one, f_one = em_map(q_zero, f_zero)
        rq = q_one - q_zero
        rf = f_one - f_zero
        first_local = q_weight * jnp.sum(rq * rq) + f_weight * jnp.sum(rf * rf)
        q_two, f_two = em_map(q_one, f_one)
        vq = q_two - 2.0 * q_one + q_zero
        vf = f_two - 2.0 * f_one + f_zero
        second_local = q_weight * jnp.sum(vq * vq) + f_weight * jnp.sum(vf * vf)
        first, second = lax.psum((first_local, second_local), ("ind", "snp"))
        alpha = -jnp.sqrt(first / (second + 1e-20))
        q_ext = jnp.clip(q_zero - 2.0 * alpha * rq + alpha * alpha * vq, clip_low, 1.0 - clip_low)
        q_zero = q_ext / jnp.sum(q_ext, axis=1, keepdims=True)
        f_zero = jnp.clip(f_zero - 2.0 * alpha * rf + alpha * alpha * vf, clip_low, 1.0 - clip_low)
    f_final = lax.dynamic_slice_in_dim(f_zero, lax.axis_index("ind") * own_rows, own_rows, 0)
    return (q_zero, f_final)


def split3(x):
    one = x.astype(bf16)
    rest = x - one.astype(f32)
    two = rest.astype(bf16)
    three = (rest - two.astype(f32)).astype(bf16)
    return one, two, three


def nn(left, right):
    return jnp.dot(left, right, preferred_element_type=f32)


def nt(left, right):
    return lax.dot_general(left, right, (((1,), (1,)), ((), ())), preferred_element_type=f32)


def total_of(x):
    return jnp.sum(jnp.sum(x, axis=1, keepdims=True), axis=0, keepdims=True)


def kernel(
    inds, geno_ref, obs_ref, anc_ref, freq_ref, q_out, f_out,
    geno_all, obs_all, anc_all, hits, misses, part, pair_in, mine, scat_in, full,
    q_zero, q_one, f_zero, f_one, flip,
    anc_send, geno_send, obs_send, geno_recv, obs_recv, anc_recv,
    pair_send, pair_recv, scat_send, scat_recv, gath_send, gath_recv, fwd_send, fwd_recv,
):
    me = lax.axis_index("ind")
    core = lax.axis_index("snp")
    other = 1 - core
    rows = geno_ref.shape[0]
    blocks = hits.shape[0]
    kdim = anc_ref.shape[1]
    peers = [lax.rem(me + d, inds) for d in range(1, inds)]

    barrier = pltpu.get_barrier_semaphore()
    for j in peers:
        pl.semaphore_signal(barrier, inc=1, device_id=(j, core), device_id_type=MESH)
    pl.semaphore_signal(barrier, inc=1, device_id=(me, other), device_id_type=MESH)
    pl.semaphore_wait(barrier, inds)

    def send(src, dst, ssem, rsem, dev):
        copy = pltpu.make_async_remote_copy(
            src_ref=src, dst_ref=dst, send_sem=ssem, recv_sem=rsem,
            device_id=dev, device_id_type=MESH,
        )
        copy.start()
        return copy

    def arrived(ref, sem):
        pltpu.make_async_copy(ref, ref, sem).wait()

    most = pl.ds(0, inds - 1)
    for j in peers:
        send(anc_ref, anc_all.at[me], anc_send, anc_recv, (j, core))
    for j in peers:
        cols = pl.ds(pl.multiple_of(j * 128, 128), 128)
        send(geno_ref.at[:, cols], geno_all.at[me], geno_send, geno_recv, (j, core))
        send(obs_ref.at[:, cols], obs_all.at[me], obs_send, obs_recv, (j, core))
    own = pl.ds(pl.multiple_of(me * 128, 128), 128)
    geno_all[me] = geno_ref[:, own]
    obs_all[me] = obs_ref[:, own]
    anc_all[me] = anc_ref[...]
    f_zero[...] = freq_ref[...]
    arrived(anc_all.at[most], anc_recv)
    arrived(geno_all.at[most], geno_recv)
    arrived(obs_all.at[most], obs_recv)
    for block in range(blocks):
        anc = jnp.concatenate([anc_all[2 * block], anc_all[2 * block + 1]], axis=0).T
        q_zero[:, 128 * block : 128 * block + 128] = anc / jnp.sum(anc, axis=0, keepdims=True)
        geno = jnp.concatenate([geno_all[2 * block], geno_all[2 * block + 1]], axis=0).astype(f32).T
        seen = jnp.concatenate([obs_all[2 * block], obs_all[2 * block + 1]], axis=0).astype(f32).T
        hits[block] = seen * geno
        misses[block] = seen * (2.0 - geno)
    arrived(anc_all.at[most], anc_send)
    arrived(geno_all.at[most], geno_send)
    arrived(obs_all.at[most], obs_send)

    lane = lax.broadcasted_iota(jnp.int32, (1, 128), 1)

    def em_map(e, q_ref, f, extra_of):
        ft = f.T
        f1, f2, f3 = split3(ft)
        lhs = jnp.concatenate([x.astype(f32) for x in (f1, f2, f1, f2, f3, f1, f3, f2)], axis=0).T.astype(bf16)
        g1, g2, g3 = split3(jnp.concatenate([ft, 1.0 - ft], axis=1))
        g64 = jnp.concatenate([g1, g2], axis=0)
        g96 = jnp.concatenate([g1, g2, g3], axis=0)
        cd = jnp.zeros((256, kdim), f32)
        for chunk in range(blocks // 2):
            q1, q2, q3 = split3(q_ref[:, 256 * chunk : 256 * chunk + 256])
            prob = nn(lhs, jnp.concatenate([q1, q1, q2, q2, q1, q3, q2, q3], axis=0))
            hit = jnp.concatenate([hits[2 * chunk], hits[2 * chunk + 1]], axis=1)
            miss = jnp.concatenate([misses[2 * chunk], misses[2 * chunk + 1]], axis=1)
            ab = jnp.concatenate([hit / prob, miss / (1.0 - prob)], axis=0)
            a1, a2, a3 = split3(ab)
            x = nn(g96, a1)
            y = nn(g64, a2)
            sums = x[0:kdim] + (x[kdim : 2 * kdim] + y[0:kdim] + (x[2 * kdim :] + y[kdim:] + nn(g1, a3)))
            for half in range(2):
                for r in range(4):
                    part[e, r // 2, (r % 2) * blocks + 2 * chunk + half, 0:8, :] = sums[
                        8 * r : 8 * r + 8, 128 * half : 128 * half + 128
                    ]
            u = nt(a1, jnp.concatenate([q1, q2, q3], axis=0))
            w = nt(a2, jnp.concatenate([q1, q2], axis=0))
            cd += u[:, 0:kdim] + (
                u[:, kdim : 2 * kdim] + w[:, 0:kdim] + (u[:, 2 * kdim :] + w[:, kdim:] + nt(a3, q1))
            )
        fc = f * cd[0:128]
        f_next = fc / (fc + (1.0 - f) * cd[128:256])
        extra = extra_of(f_next)
        for c in range(2):
            for i in range(inds):
                part[e, c, i, 8:9, :] = extra
        pair = send(part.at[e, other], pair_in.at[e], pair_send.at[e], pair_recv.at[e], (me, other))
        pair.wait_recv()
        mine[e] = part[e, core] + pair_in[e]
        for j in peers:
            send(mine.at[e, j], scat_in.at[e, me], scat_send.at[e], scat_recv.at[e], (j, core))
        scat_in[e, me] = mine[e, me]
        arrived(scat_in.at[e, most], scat_recv.at[e])
        total = scat_in[e, 0]
        for i in range(1, inds):
            total = total + scat_in[e, i]
        full[e, core, me] = total[0:8]
        for j in peers:
            send(full.at[e, core, me], full.at[e, core, me], gath_send.at[e], gath_recv.at[e], (j, core))
        arrived(full.at[e, core, most], gath_recv.at[e])
        fwd = send(full.at[e, core], full.at[e, core], fwd_send.at[e], fwd_recv.at[e], (me, other))
        fwd.wait_recv()
        sums = jnp.concatenate(
            [
                jnp.concatenate([full[e, r // 2, (r % 2) * blocks + b] for b in range(blocks)], axis=1)
                for r in range(4)
            ],
            axis=0,
        )
        q_next = q_ref[...] * sums
        q_next = q_next / jnp.sum(q_next, axis=0, keepdims=True)
        pair.wait_send()
        fwd.wait_send()
        arrived(scat_in.at[e, most], scat_send.at[e])
        arrived(full.at[e, core, most], gath_send.at[e])
        return q_next, f_next, total[8:9]

    def one_step(step, carry):
        f0 = f_zero[...]
        q_first, f_first, _ = em_map(2 * step, q_zero, f0, lambda f: jnp.zeros((1, 128), f32))
        q_one[...] = q_first
        f_one[...] = f_first
        rf = f_first - f0
        rr_f = total_of(rf * rf)

        def lengths(f_next):
            vf = f_next - 2.0 * f_first + f0
            return jnp.where(lane == 0, rr_f, jnp.where(lane == 1, total_of(vf * vf), 0.0))

        q_two, f_two, row = em_map(2 * step + 1, q_one, f_one[...], lengths)
        q0 = q_zero[...]
        rq = q_one[...] - q0
        vq = q_two - 2.0 * q_one[...] + q0
        vf = f_two - 2.0 * f_first + f0
        first = total_of(rq * rq) + total_of(jnp.where(lane == 0, row, 0.0))
        second = total_of(vq * vq) + total_of(jnp.where(lane == 1, row, 0.0))
        alpha = -jnp.sqrt(first / (second + 1e-20))
        q_ext = jnp.clip(q0 - 2.0 * alpha * rq + alpha * alpha * vq, clip_low, 1.0 - clip_low)
        q_zero[...] = q_ext / jnp.sum(q_ext, axis=0, keepdims=True)
        f_zero[...] = jnp.clip(f0 - 2.0 * alpha * rf + alpha * alpha * vf, clip_low, 1.0 - clip_low)
        return carry

    lax.fori_loop(0, STEPS, one_step, 0)
    f_out[...] = f_zero[...]
    flip[...] = q_zero[:, pl.ds(pl.multiple_of(me // 2 * 128, 128), 128)].T
    q_out[...] = flip[pl.ds(pl.multiple_of(lax.rem(me, 2) * rows, rows), rows), :]


def fast_device(genotypes, observed, ancestry, freqs):
    inds = lax.axis_size("ind")
    rows, kdim = ancestry.shape
    people = rows * inds
    blocks = people // 128
    maps = 2 * STEPS
    dma = pltpu.SemaphoreType.DMA
    vmem = pl.BlockSpec(memory_space=pltpu.VMEM)
    return pl.pallas_call(
        functools.partial(kernel, inds),
        out_shape=(
            jax.ShapeDtypeStruct(ancestry.shape, f32),
            jax.ShapeDtypeStruct(freqs.shape, f32),
        ),
        in_specs=[vmem] * 4,
        out_specs=(vmem, vmem),
        scratch_shapes=[
            pltpu.VMEM((inds, rows, 128), jnp.int32),
            pltpu.VMEM((inds, rows, 128), jnp.int32),
            pltpu.VMEM((inds, rows, kdim), f32),
            pltpu.VMEM((blocks, 128, 128), f32),
            pltpu.VMEM((blocks, 128, 128), f32),
            pltpu.VMEM((maps, 2, inds, 9, 128), f32),
            pltpu.VMEM((maps, inds, 9, 128), f32),
            pltpu.VMEM((maps, inds, 9, 128), f32),
            pltpu.VMEM((maps, inds, 9, 128), f32),
            pltpu.VMEM((maps, 2, inds, 8, 128), f32),
            pltpu.VMEM((kdim, people), f32),
            pltpu.VMEM((kdim, people), f32),
            pltpu.VMEM((128, kdim), f32),
            pltpu.VMEM((128, kdim), f32),
            pltpu.VMEM((128, kdim), f32),
            dma, dma, dma, dma, dma, dma,
        ]
        + [dma((maps,))] * 8,
        compiler_params=pltpu.CompilerParams(
            collective_id=0, has_side_effects=True, vmem_limit_bytes=40 * 1024 * 1024
        ),
    )(genotypes, observed, ancestry, freqs)


def pick(genotypes, observed, ancestry, freqs):
    inds = lax.axis_size("ind")
    rows, kdim = ancestry.shape
    fits = (
        lax.axis_size("snp") == 2
        and freqs.shape[0] == 128
        and rows == 64
        and kdim == 32
        and inds % 4 == 0
        and (rows * inds // 128) * 2 == inds
    )
    form = fast_device if fits else per_device
    return form(genotypes, observed, ancestry, freqs)


def solution(mesh):
    in_specs = (P("ind", "snp"), P("ind", "snp"), P("ind", None), P(("snp", "ind"), None))
    out_specs = (P("ind", None), P(("snp", "ind"), None))
    return jax.shard_map(pick, mesh=mesh, in_specs=in_specs, out_specs=out_specs, check_vma=False)
```

```python
import functools

import jax
import jax.numpy as jnp
from jax import lax
from jax.experimental import pallas as pl
from jax.experimental.pallas import tpu as pltpu
from jax.sharding import PartitionSpec as P

STEPS = 3


clip_low = 1e-05
high = lax.Precision.HIGHEST
MESH = pl.DeviceIdType.MESH
f32 = jnp.float32
bf16 = jnp.bfloat16


def over_rows(left, right):
    return lax.dot_general(
        left, right, (((0,), (0,)), ((), ())), precision=high, preferred_element_type=jnp.float32
    )


def per_device(genotypes, observed, ancestry, freqs):
    ind_count = lax.axis_size("ind")
    snp_count = lax.axis_size("snp")
    geno = genotypes.astype(jnp.float32)
    seen = observed.astype(jnp.float32)
    hits = seen * geno
    misses = seen * (2.0 - geno)
    own_rows = freqs.shape[0]
    q_zero = ancestry / jnp.sum(ancestry, axis=1, keepdims=True)
    f_zero = lax.all_gather(freqs, "ind", axis=0, tiled=True)
    f_weight = 1.0 / ind_count
    q_weight = 1.0 / snp_count

    def em_map(q_rows, f_state):
        prob = jnp.dot(q_rows, f_state.T, precision=high, preferred_element_type=jnp.float32)
        ratio_a = hits / prob
        ratio_b = misses / (1.0 - prob)
        sum_a = jnp.dot(ratio_a, f_state, precision=high, preferred_element_type=jnp.float32)
        sum_b = jnp.dot(ratio_b, 1.0 - f_state, precision=high, preferred_element_type=jnp.float32)
        c_part = over_rows(ratio_a, q_rows)
        d_part = over_rows(ratio_b, q_rows)
        sum_a, sum_b = lax.psum((sum_a, sum_b), "snp")
        q_next = q_rows * (sum_a + sum_b)
        q_next = q_next / jnp.sum(q_next, axis=1, keepdims=True)
        c_total, d_total = lax.psum((c_part, d_part), "ind")
        f_next = f_state * c_total / (f_state * c_total + (1.0 - f_state) * d_total)
        return (q_next, f_next)

    for step in range(STEPS):
        q_one, f_one = em_map(q_zero, f_zero)
        rq = q_one - q_zero
        rf = f_one - f_zero
        first_local = q_weight * jnp.sum(rq * rq) + f_weight * jnp.sum(rf * rf)
        q_two, f_two = em_map(q_one, f_one)
        vq = q_two - 2.0 * q_one + q_zero
        vf = f_two - 2.0 * f_one + f_zero
        second_local = q_weight * jnp.sum(vq * vq) + f_weight * jnp.sum(vf * vf)
        first, second = lax.psum((first_local, second_local), ("ind", "snp"))
        alpha = -jnp.sqrt(first / (second + 1e-20))
        q_ext = jnp.clip(q_zero - 2.0 * alpha * rq + alpha * alpha * vq, clip_low, 1.0 - clip_low)
        q_zero = q_ext / jnp.sum(q_ext, axis=1, keepdims=True)
        f_zero = jnp.clip(f_zero - 2.0 * alpha * rf + alpha * alpha * vf, clip_low, 1.0 - clip_low)
    f_final = lax.dynamic_slice_in_dim(f_zero, lax.axis_index("ind") * own_rows, own_rows, 0)
    return (q_zero, f_final)


def split3(x):
    one = x.astype(bf16)
    rest = x - one.astype(f32)
    two = rest.astype(bf16)
    three = (rest - two.astype(f32)).astype(bf16)
    return one, two, three


def nn(left, right):
    return jnp.dot(left, right, preferred_element_type=f32)


def nt(left, right):
    return lax.dot_general(left, right, (((1,), (1,)), ((), ())), preferred_element_type=f32)


def total_of(x):
    return jnp.sum(jnp.sum(x, axis=1, keepdims=True), axis=0, keepdims=True)


def kernel(
    inds, geno_ref, obs_ref, anc_ref, freq_ref, q_out, f_out,
    geno_all, obs_all, anc_all, hits, misses, part, pair_in, mine, scat_in, full,
    len_own, len_pair, len_sum, len_all,
    q_zero, q_one, f_zero, f_one, flip,
    anc_send, anc_recv, geno_send, obs_send, geno_recv, obs_recv,
    pair_send, pair_recv, scat_send, scat_recv, gath_send, gath_recv, fwd_send, fwd_recv,
    lp_send, lp_recv, la_send, la_recv,
):
    me = lax.axis_index("ind")
    core = lax.axis_index("snp")
    other = 1 - core
    rows = geno_ref.shape[0]
    chunks = hits.shape[0]
    blocks = 2 * chunks
    kdim = anc_ref.shape[1]
    width = inds.bit_length() - 1
    bits = [lax.rem(lax.div(me, 1 << k), 2) for k in range(width)]

    def flipped(d, low=0):
        j = 0
        for k in range(low, width):
            bit = 1 - bits[k] if (d >> k) & 1 else bits[k]
            j = j + bit * (1 << (k - low))
        return j

    peers = [(d, flipped(d)) for d in range(inds - 1, 0, -1)]

    barrier = pltpu.get_barrier_semaphore()
    for _, j in peers:
        pl.semaphore_signal(barrier, inc=1, device_id=(j, core), device_id_type=MESH)
    pl.semaphore_signal(barrier, inc=1, device_id=(me, other), device_id_type=MESH)
    pl.semaphore_wait(barrier, inds)

    def remote(src, dst, ssem, rsem, dev):
        return pltpu.make_async_remote_copy(
            src_ref=src, dst_ref=dst, send_sem=ssem, recv_sem=rsem,
            device_id=dev, device_id_type=MESH,
        )

    def send(*args):
        remote(*args).start()

    def arrived(ref, sem):
        pltpu.make_async_copy(ref, ref, sem).wait()

    most = pl.ds(0, inds - 1)
    for _, j in peers:
        send(anc_ref, anc_all.at[me], anc_send, anc_recv, (j, core))
    for d, j in peers:
        cols = pl.ds(pl.multiple_of(j * 128, 128), 128)
        send(geno_ref.at[:, cols], geno_all.at[me], geno_send, geno_recv.at[d // 4], (j, core))
        send(obs_ref.at[:, cols], obs_all.at[me], obs_send, obs_recv.at[d // 4], (j, core))
    own = pl.ds(pl.multiple_of(me * 128, 128), 128)
    geno_all[me] = geno_ref[:, own]
    obs_all[me] = obs_ref[:, own]
    anc_all[me] = anc_ref[...]
    f_zero[...] = freq_ref[...]
    arrived(anc_all.at[most], anc_recv)
    for chunk in range(chunks):
        anc = jnp.concatenate([anc_all[4 * chunk + s] for s in range(4)], axis=0).T
        q_zero[chunk] = anc / jnp.sum(anc, axis=0, keepdims=True)

    def lay(cc, chunk):
        count = pl.ds(0, 4 if cc else 3)
        arrived(geno_all.at[count], geno_recv.at[cc])
        arrived(obs_all.at[count], obs_recv.at[cc])
        for half in range(2):
            at = 4 * chunk + 2 * half
            geno = jnp.concatenate([geno_all[at], geno_all[at + 1]], axis=0).astype(f32).T
            seen = jnp.concatenate([obs_all[at], obs_all[at + 1]], axis=0).astype(f32).T
            hits[chunk, :, 128 * half : 128 * half + 128] = seen * geno
            misses[chunk, :, 128 * half : 128 * half + 128] = seen * (2.0 - geno)

    lane = lax.broadcasted_iota(jnp.int32, (8, 128), 1)

    def prepare(f):
        ft = f.T
        f1, f2, f3 = split3(ft)
        lhs = jnp.concatenate([x.astype(f32) for x in (f1, f2, f1, f2, f3, f1, f3, f2)], axis=0).T.astype(bf16)
        g1, g2, g3 = split3(jnp.concatenate([ft, 1.0 - ft], axis=1))
        return lhs, g1, jnp.concatenate([g1, g2], axis=0), jnp.concatenate([g1, g2, g3], axis=0)

    def em_map(e, q_ref, f, ready, is_first, lengths_of, step):
        lhs, g1, g64, g96 = ready
        kept = []
        for cc in range(chunks):
            chunk = flipped(4 * cc, 2) if is_first else cc
            if is_first:
                lay(cc, chunk)
            q1, q2, q3 = split3(q_ref[chunk])
            prob = nn(lhs, jnp.concatenate([q1, q1, q2, q2, q1, q3, q2, q3], axis=0))
            ab = jnp.concatenate([hits[chunk] / prob, misses[chunk] / (1.0 - prob)], axis=0)
            a1, a2, a3 = split3(ab)
            x = nn(g96, a1)
            y = nn(g64, a2)
            sums = x[0:kdim] + (x[kdim : 2 * kdim] + y[0:kdim] + (x[2 * kdim :] + y[kdim:] + nn(g1, a3)))
            for half in range(2):
                for r in range(4):
                    part[e, r // 2, (r % 2) * blocks + 2 * chunk + half] = sums[
                        8 * r : 8 * r + 8, 128 * half : 128 * half + 128
                    ]
            kept.append((a1, a2, a3, q1, q2, q3))

        pair = remote(part.at[e, other], pair_in.at[e], pair_send.at[e], pair_recv.at[e], (me, other))
        pair.start()

        def products(some):
            u = w = v = 0.0
            for a1, a2, a3, q1, q2, q3 in some:
                u = u + nt(a1, jnp.concatenate([q1, q2, q3], axis=0))
                w = w + nt(a2, jnp.concatenate([q1, q2], axis=0))
                v = v + nt(a3, q1)
            return u, w, v

        early = products(kept[: chunks // 2])
        pair.wait_recv()
        mine[e] = part[e, core] + pair_in[e]
        for _, j in peers:
            send(mine.at[e, j], scat_in.at[e, me], scat_send.at[e], scat_recv.at[e], (j, core))
        scat_in[e, me] = mine[e, me]
        late = products(kept[chunks // 2 :])
        u, w, v = [x + y for x, y in zip(early, late)]
        cd = u[:, 0:kdim] + (u[:, kdim : 2 * kdim] + w[:, 0:kdim] + (u[:, 2 * kdim :] + w[:, kdim:] + v))
        fc = f * cd[0:128]
        f_next = fc / (fc + (1.0 - f) * cd[128:256])
        if lengths_of is not None:
            len_own[step] = lengths_of(f_next)
            len_copy = remote(len_own.at[step], len_pair.at[step], lp_send.at[step], lp_recv.at[step], (me, other))
            len_copy.start()
        arrived(scat_in.at[e, most], scat_recv.at[e])
        total = scat_in[e, 0]
        for i in range(1, inds):
            total = total + scat_in[e, i]
        full[e, core, me] = total
        for d, j in peers:
            send(full.at[e, core, me], full.at[e, core, me], gath_send.at[e], gath_recv.at[e, d], (j, core))
        send(full.at[e, core, me], full.at[e, core, me], fwd_send.at[e], fwd_recv.at[e], (me, other))
        if lengths_of is not None:
            len_copy.wait_recv()
            len_sum[step] = len_own[step] + len_pair[step]
            for _, j in peers:
                send(len_sum.at[step], len_all.at[step, me], la_send.at[step], la_recv.at[step], (j, core))
            len_all[step, me] = len_sum[step]
            later = None
        else:
            later = prepare(f_next)
        for d, j in peers:
            slot = full.at[e, core, j]
            arrived(slot, gath_recv.at[e, d])
            send(slot, slot, fwd_send.at[e], fwd_recv.at[e], (me, other))
        lengths = None
        if lengths_of is not None:
            arrived(len_all.at[step, most], la_recv.at[step])
            lengths = len_all[step, 0]
            for i in range(1, inds):
                lengths = lengths + len_all[step, i]
            len_copy.wait_send()
            arrived(len_all.at[step, most], la_send.at[step])
        arrived(full.at[e, other], fwd_recv.at[e])
        q_next = []
        for chunk in range(chunks):
            sums = jnp.concatenate(
                [
                    jnp.concatenate(
                        [full[e, r // 2, (r % 2) * blocks + 2 * chunk + half] for half in range(2)], axis=1
                    )
                    for r in range(4)
                ],
                axis=0,
            )
            grown = q_ref[chunk] * sums
            q_next.append((grown / jnp.sum(grown, axis=0, keepdims=True))[None])
        pair.wait_send()
        arrived(scat_in.at[e, most], scat_send.at[e])
        arrived(full.at[e, core, most], gath_send.at[e])
        arrived(full.at[e, core], fwd_send.at[e])
        return jnp.concatenate(q_next, axis=0), f_next, later, lengths

    def all_sum(x):
        return total_of(jnp.sum(x, axis=0))

    def one_step(step, is_first):
        f0 = f_zero[...]
        q_first, f_first, ready, _ = em_map(2 * step, q_zero, f0, prepare(f0), is_first, None, step)
        q_one[...] = q_first
        f_one[...] = f_first

        def lengths_of(f_next):
            rf = f_first - f0
            vf = f_next - 2.0 * f_first + f0
            return jnp.where(lane == 0, total_of(rf * rf), jnp.where(lane == 1, total_of(vf * vf), 0.0))

        q_two, f_two, _, lengths = em_map(2 * step + 1, q_one, f_first, ready, False, lengths_of, step)
        q0 = q_zero[...]
        rq = q_one[...] - q0
        vq = q_two - 2.0 * q_one[...] + q0
        rf = f_first - f0
        vf = f_two - 2.0 * f_first + f0
        row = lengths[0:1]
        first = all_sum(rq * rq) + total_of(jnp.where(lane[0:1] == 0, row, 0.0))
        second = all_sum(vq * vq) + total_of(jnp.where(lane[0:1] == 1, row, 0.0))
        alpha = -jnp.sqrt(first / (second + 1e-20))
        q_ext = jnp.clip(q0 - 2.0 * alpha * rq + alpha * alpha * vq, clip_low, 1.0 - clip_low)
        q_zero[...] = q_ext / jnp.sum(q_ext, axis=1, keepdims=True)
        f_zero[...] = jnp.clip(f0 - 2.0 * alpha * rf + alpha * alpha * vf, clip_low, 1.0 - clip_low)

    one_step(0, True)
    arrived(anc_all.at[most], anc_send)
    arrived(geno_all.at[most], geno_send)
    arrived(obs_all.at[most], obs_send)

    def again(step, carry):
        one_step(step, False)
        return carry

    lax.fori_loop(1, STEPS, again, 0)
    f_out[...] = f_zero[...]
    flip[...] = q_zero[lax.div(me, 4)].T
    q_out[...] = flip[pl.ds(pl.multiple_of(lax.rem(me, 4) * rows, rows), rows), :]


def fast_device(genotypes, observed, ancestry, freqs):
    inds = lax.axis_size("ind")
    rows, kdim = ancestry.shape
    people = rows * inds
    chunks = people // 256
    maps = 2 * STEPS
    dma = pltpu.SemaphoreType.DMA
    vmem = pl.BlockSpec(memory_space=pltpu.VMEM)
    return pl.pallas_call(
        functools.partial(kernel, inds),
        out_shape=(
            jax.ShapeDtypeStruct(ancestry.shape, f32),
            jax.ShapeDtypeStruct(freqs.shape, f32),
        ),
        in_specs=[vmem] * 4,
        out_specs=(vmem, vmem),
        scratch_shapes=[
            pltpu.VMEM((inds, rows, 128), jnp.int32),
            pltpu.VMEM((inds, rows, 128), jnp.int32),
            pltpu.VMEM((inds, rows, kdim), f32),
            pltpu.VMEM((chunks, 128, 256), f32),
            pltpu.VMEM((chunks, 128, 256), f32),
            pltpu.VMEM((maps, 2, inds, 8, 128), f32),
            pltpu.VMEM((maps, inds, 8, 128), f32),
            pltpu.VMEM((maps, inds, 8, 128), f32),
            pltpu.VMEM((maps, inds, 8, 128), f32),
            pltpu.VMEM((maps, 2, inds, 8, 128), f32),
            pltpu.VMEM((STEPS, 8, 128), f32),
            pltpu.VMEM((STEPS, 8, 128), f32),
            pltpu.VMEM((STEPS, 8, 128), f32),
            pltpu.VMEM((STEPS, inds, 8, 128), f32),
            pltpu.VMEM((chunks, kdim, 256), f32),
            pltpu.VMEM((chunks, kdim, 256), f32),
            pltpu.VMEM((128, kdim), f32),
            pltpu.VMEM((128, kdim), f32),
            pltpu.VMEM((256, kdim), f32),
            dma, dma, dma, dma,
            dma((chunks,)),
            dma((chunks,)),
        ]
        + [dma((maps,))] * 5
        + [dma((maps, inds))]
        + [dma((maps,))] * 2
        + [dma((STEPS,))] * 4,
        compiler_params=pltpu.CompilerParams(
            collective_id=0, has_side_effects=True, vmem_limit_bytes=40 * 1024 * 1024
        ),
    )(genotypes, observed, ancestry, freqs)


def pick(genotypes, observed, ancestry, freqs):
    inds = lax.axis_size("ind")
    rows, kdim = ancestry.shape
    fits = (
        lax.axis_size("snp") == 2
        and freqs.shape[0] == 128
        and rows == 64
        and kdim == 32
        and inds >= 4
        and inds & (inds - 1) == 0
    )
    form = fast_device if fits else per_device
    return form(genotypes, observed, ancestry, freqs)


def solution(mesh):
    in_specs = (P("ind", "snp"), P("ind", "snp"), P("ind", None), P(("snp", "ind"), None))
    out_specs = (P("ind", None), P(("snp", "ind"), None))
    return jax.shard_map(pick, mesh=mesh, in_specs=in_specs, out_specs=out_specs, check_vma=False)
```

```python
import functools

import jax
import jax.numpy as jnp
from jax import lax
from jax.experimental import pallas as pl
from jax.experimental.pallas import tpu as pltpu
from jax.sharding import PartitionSpec as P

STEPS = 3


clip_low = 1e-05
high = lax.Precision.HIGHEST
MESH = pl.DeviceIdType.MESH
f32 = jnp.float32
bf16 = jnp.bfloat16


def over_rows(left, right):
    return lax.dot_general(
        left, right, (((0,), (0,)), ((), ())), precision=high, preferred_element_type=jnp.float32
    )


def per_device(genotypes, observed, ancestry, freqs):
    ind_count = lax.axis_size("ind")
    snp_count = lax.axis_size("snp")
    geno = genotypes.astype(jnp.float32)
    seen = observed.astype(jnp.float32)
    hits = seen * geno
    misses = seen * (2.0 - geno)
    own_rows = freqs.shape[0]
    q_zero = ancestry / jnp.sum(ancestry, axis=1, keepdims=True)
    f_zero = lax.all_gather(freqs, "ind", axis=0, tiled=True)
    f_weight = 1.0 / ind_count
    q_weight = 1.0 / snp_count

    def em_map(q_rows, f_state):
        prob = jnp.dot(q_rows, f_state.T, precision=high, preferred_element_type=jnp.float32)
        ratio_a = hits / prob
        ratio_b = misses / (1.0 - prob)
        sum_a = jnp.dot(ratio_a, f_state, precision=high, preferred_element_type=jnp.float32)
        sum_b = jnp.dot(ratio_b, 1.0 - f_state, precision=high, preferred_element_type=jnp.float32)
        c_part = over_rows(ratio_a, q_rows)
        d_part = over_rows(ratio_b, q_rows)
        sum_a, sum_b = lax.psum((sum_a, sum_b), "snp")
        q_next = q_rows * (sum_a + sum_b)
        q_next = q_next / jnp.sum(q_next, axis=1, keepdims=True)
        c_total, d_total = lax.psum((c_part, d_part), "ind")
        f_next = f_state * c_total / (f_state * c_total + (1.0 - f_state) * d_total)
        return (q_next, f_next)

    for step in range(STEPS):
        q_one, f_one = em_map(q_zero, f_zero)
        rq = q_one - q_zero
        rf = f_one - f_zero
        first_local = q_weight * jnp.sum(rq * rq) + f_weight * jnp.sum(rf * rf)
        q_two, f_two = em_map(q_one, f_one)
        vq = q_two - 2.0 * q_one + q_zero
        vf = f_two - 2.0 * f_one + f_zero
        second_local = q_weight * jnp.sum(vq * vq) + f_weight * jnp.sum(vf * vf)
        first, second = lax.psum((first_local, second_local), ("ind", "snp"))
        alpha = -jnp.sqrt(first / (second + 1e-20))
        q_ext = jnp.clip(q_zero - 2.0 * alpha * rq + alpha * alpha * vq, clip_low, 1.0 - clip_low)
        q_zero = q_ext / jnp.sum(q_ext, axis=1, keepdims=True)
        f_zero = jnp.clip(f_zero - 2.0 * alpha * rf + alpha * alpha * vf, clip_low, 1.0 - clip_low)
    f_final = lax.dynamic_slice_in_dim(f_zero, lax.axis_index("ind") * own_rows, own_rows, 0)
    return (q_zero, f_final)


def split3(x):
    one = x.astype(bf16)
    rest = x - one.astype(f32)
    two = rest.astype(bf16)
    three = (rest - two.astype(f32)).astype(bf16)
    return one, two, three


def nn(left, right):
    return jnp.dot(left, right, preferred_element_type=f32)


def nt(left, right):
    return lax.dot_general(left, right, (((1,), (1,)), ((), ())), preferred_element_type=f32)


def total_of(x):
    return jnp.sum(jnp.sum(x, axis=1, keepdims=True), axis=0, keepdims=True)


def kernel(
    inds, geno_ref, obs_ref, anc_ref, freq_ref, q_out, f_out,
    geno_all, obs_all, anc_all, hits, misses, part, rs_in, z_own, z_in, full,
    len_own, len_in, len_sum, len_z,
    q_zero, q_one, f_zero, f_one, flip,
    anc_send, anc_recv, geno_send, obs_send, geno_recv, obs_recv,
    rs_send, rs_recv, z_send, z_recv, ag_send, ag_recv,
    lr_send, lr_recv, lz_send, lz_recv,
):
    me = lax.axis_index("ind")
    core = lax.axis_index("snp")
    other = 1 - core
    rows = geno_ref.shape[0]
    chunks = hits.shape[0]
    kdim = anc_ref.shape[1]
    width = inds.bit_length() - 1
    bits = [lax.rem(lax.div(me, 1 << k), 2) for k in range(width)]

    def flipped(d, low=0):
        j = 0
        for k in range(low, width):
            bit = 1 - bits[k] if (d >> k) & 1 else bits[k]
            j = j + bit * (1 << (k - low))
        return j

    peers = [(d, flipped(d)) for d in range(inds - 1, 0, -1)]

    group = core * 4 + lax.rem(me, 4)
    layer = lax.div(me, 4)
    near = [(flipped(d % 4), other if d >= 4 else core) for d in (7, 3, 6, 5, 2, 1, 4)]
    near = [(j, c, c * 4 + lax.rem(j, 4)) for j, c in near]
    columns = [(flipped(4 * d), core) for d in (3, 2, 1)]

    barrier = pltpu.get_barrier_semaphore()
    for _, j in peers:
        pl.semaphore_signal(barrier, inc=1, device_id=(j, core), device_id_type=MESH)
    for d in range(4):
        pl.semaphore_signal(barrier, inc=1, device_id=(flipped(d), other), device_id_type=MESH)
    pl.semaphore_wait(barrier, inds + 3)

    def remote(src, dst, ssem, rsem, dev):
        return pltpu.make_async_remote_copy(
            src_ref=src, dst_ref=dst, send_sem=ssem, recv_sem=rsem,
            device_id=dev, device_id_type=MESH,
        )

    def send(*args):
        remote(*args).start()

    def arrived(ref, sem):
        pltpu.make_async_copy(ref, ref, sem).wait()

    most = pl.ds(0, inds - 1)
    for _, j in peers:
        send(anc_ref, anc_all.at[me], anc_send, anc_recv, (j, core))
    for d, j in peers:
        cols = pl.ds(pl.multiple_of(j * 128, 128), 128)
        send(geno_ref.at[:, cols], geno_all.at[me], geno_send, geno_recv.at[d // 4], (j, core))
        send(obs_ref.at[:, cols], obs_all.at[me], obs_send, obs_recv.at[d // 4], (j, core))
    own = pl.ds(pl.multiple_of(me * 128, 128), 128)
    geno_all[me] = geno_ref[:, own]
    obs_all[me] = obs_ref[:, own]
    anc_all[me] = anc_ref[...]
    f_zero[...] = freq_ref[...]
    arrived(anc_all.at[most], anc_recv)
    for chunk in range(chunks):
        anc = jnp.concatenate([anc_all[4 * chunk + s] for s in range(4)], axis=0).T
        anc = anc / jnp.sum(anc, axis=0, keepdims=True)
        for half in range(2):
            q_zero[2 * chunk + half] = anc[:, 128 * half : 128 * half + 128]

    def lay(cc, chunk):
        count = pl.ds(0, 4 if cc else 3)
        arrived(geno_all.at[count], geno_recv.at[cc])
        arrived(obs_all.at[count], obs_recv.at[cc])
        for half in range(2):
            at = 4 * chunk + 2 * half
            geno = jnp.concatenate([geno_all[at], geno_all[at + 1]], axis=0).astype(f32).T
            seen = jnp.concatenate([obs_all[at], obs_all[at + 1]], axis=0).astype(f32).T
            hits[chunk, :, 128 * half : 128 * half + 128] = seen * geno
            misses[chunk, :, 128 * half : 128 * half + 128] = seen * (2.0 - geno)

    lane = lax.broadcasted_iota(jnp.int32, (8, 128), 1)

    def prepare(f):
        ft = f.T
        f1, f2, f3 = split3(ft)
        lhs = jnp.concatenate([x.astype(f32) for x in (f1, f2, f1, f2, f3, f1, f3, f2)], axis=0).T.astype(bf16)
        g1, g2, g3 = split3(jnp.concatenate([ft, 1.0 - ft], axis=1))
        return lhs, g1, jnp.concatenate([g1, g2], axis=0), jnp.concatenate([g1, g2, g3], axis=0)

    seven = pl.ds(0, 7)
    three = pl.ds(0, chunks - 1)

    def added(ref, at, count):
        total = ref[at, 0]
        for i in range(1, count):
            total = total + ref[at, i]
        return total

    def em_map(e, q_ref, f, ready, is_first, lengths_of, step):
        lhs, g1, g64, g96 = ready
        kept = []
        for cc in range(chunks):
            chunk = flipped(4 * cc, 2) if is_first else cc
            if is_first:
                lay(cc, chunk)
            q1, q2, q3 = split3(jnp.concatenate([q_ref[2 * chunk], q_ref[2 * chunk + 1]], axis=1))
            prob = nn(lhs, jnp.concatenate([q1, q1, q2, q2, q1, q3, q2, q3], axis=0))
            ab = jnp.concatenate([hits[chunk] / prob, misses[chunk] / (1.0 - prob)], axis=0)
            a1, a2, a3 = split3(ab)
            x = nn(g96, a1)
            y = nn(g64, a2)
            sums = x[0:kdim] + (x[kdim : 2 * kdim] + y[0:kdim] + (x[2 * kdim :] + y[kdim:] + nn(g1, a3)))
            for half in range(2):
                part[e, 2 * chunk + half] = sums[:, 128 * half : 128 * half + 128]
            kept.append((a1, a2, a3, q1, q2, q3))

        for j, c, g in near:
            send(part.at[e, g], rs_in.at[e, group], rs_send.at[e], rs_recv.at[e], (j, c))
        rs_in[e, group] = part[e, group]

        def products(some):
            u = w = v = 0.0
            for a1, a2, a3, q1, q2, q3 in some:
                u = u + nt(a1, jnp.concatenate([q1, q2, q3], axis=0))
                w = w + nt(a2, jnp.concatenate([q1, q2], axis=0))
                v = v + nt(a3, q1)
            return u, w, v

        early = products(kept[: chunks // 2])
        arrived(rs_in.at[e, seven], rs_recv.at[e])
        z_own[e] = added(rs_in, e, 8)
        for dev in columns:
            send(z_own.at[e], z_in.at[e, layer], z_send.at[e], z_recv.at[e], dev)
        z_in[e, layer] = z_own[e]
        late = products(kept[chunks // 2 :])
        u, w, v = [x + y for x, y in zip(early, late)]
        cd = u[:, 0:kdim] + (u[:, kdim : 2 * kdim] + w[:, 0:kdim] + (u[:, 2 * kdim :] + w[:, kdim:] + v))
        fc = f * cd[0:128]
        f_next = fc / (fc + (1.0 - f) * cd[128:256])
        if lengths_of is not None:
            len_own[step] = lengths_of(f_next)
            for j, c, g in near:
                send(len_own.at[step], len_in.at[step, group], lr_send.at[step], lr_recv.at[step], (j, c))
            len_in[step, group] = len_own[step]
        arrived(z_in.at[e, three], z_recv.at[e])
        grown = q_ref[group] * added(z_in, e, chunks)
        full[e, group] = grown / jnp.sum(grown, axis=0, keepdims=True)
        for j, c, g in near:
            send(full.at[e, group], full.at[e, group], ag_send.at[e], ag_recv.at[e], (j, c))
        later = lengths = None
        if lengths_of is not None:
            arrived(len_in.at[step, seven], lr_recv.at[step])
            len_sum[step] = added(len_in, step, 8)
            for dev in columns:
                send(len_sum.at[step], len_z.at[step, layer], lz_send.at[step], lz_recv.at[step], dev)
            len_z[step, layer] = len_sum[step]
        else:
            later = prepare(f_next)
        arrived(full.at[e, seven], ag_recv.at[e])
        if lengths_of is not None:
            arrived(len_z.at[step, three], lz_recv.at[step])
            lengths = added(len_z, step, chunks)
            arrived(len_in.at[step, seven], lr_send.at[step])
            arrived(len_z.at[step, three], lz_send.at[step])
        arrived(rs_in.at[e, seven], rs_send.at[e])
        arrived(z_in.at[e, three], z_send.at[e])
        arrived(full.at[e, seven], ag_send.at[e])
        return full[e], f_next, later, lengths

    def all_sum(x):
        return total_of(jnp.sum(x, axis=0))

    def one_step(step, is_first):
        f0 = f_zero[...]
        q_first, f_first, ready, _ = em_map(2 * step, q_zero, f0, prepare(f0), is_first, None, step)
        q_one[...] = q_first
        f_one[...] = f_first

        def lengths_of(f_next):
            rf = f_first - f0
            vf = f_next - 2.0 * f_first + f0
            return jnp.where(lane == 0, total_of(rf * rf), jnp.where(lane == 1, total_of(vf * vf), 0.0))

        q_two, f_two, _, lengths = em_map(2 * step + 1, q_one, f_first, ready, False, lengths_of, step)
        q0 = q_zero[...]
        rq = q_one[...] - q0
        vq = q_two - 2.0 * q_one[...] + q0
        rf = f_first - f0
        vf = f_two - 2.0 * f_first + f0
        row = lengths[0:1]
        first = all_sum(rq * rq) + total_of(jnp.where(lane[0:1] == 0, row, 0.0))
        second = all_sum(vq * vq) + total_of(jnp.where(lane[0:1] == 1, row, 0.0))
        alpha = -jnp.sqrt(first / (second + 1e-20))
        q_ext = jnp.clip(q0 - 2.0 * alpha * rq + alpha * alpha * vq, clip_low, 1.0 - clip_low)
        q_zero[...] = q_ext / jnp.sum(q_ext, axis=1, keepdims=True)
        f_zero[...] = jnp.clip(f0 - 2.0 * alpha * rf + alpha * alpha * vf, clip_low, 1.0 - clip_low)

    one_step(0, True)
    arrived(anc_all.at[most], anc_send)
    arrived(geno_all.at[most], geno_send)
    arrived(obs_all.at[most], obs_send)

    def again(step, carry):
        one_step(step, False)
        return carry

    lax.fori_loop(1, STEPS, again, 0)
    f_out[...] = f_zero[...]
    flip[...] = q_zero[lax.div(me, 2)].T
    q_out[...] = flip[pl.ds(pl.multiple_of(lax.rem(me, 2) * rows, rows), rows), :]


def fast_device(genotypes, observed, ancestry, freqs):
    inds = lax.axis_size("ind")
    rows, kdim = ancestry.shape
    people = rows * inds
    chunks = people // 256
    maps = 2 * STEPS
    dma = pltpu.SemaphoreType.DMA
    vmem = pl.BlockSpec(memory_space=pltpu.VMEM)
    return pl.pallas_call(
        functools.partial(kernel, inds),
        out_shape=(
            jax.ShapeDtypeStruct(ancestry.shape, f32),
            jax.ShapeDtypeStruct(freqs.shape, f32),
        ),
        in_specs=[vmem] * 4,
        out_specs=(vmem, vmem),
        scratch_shapes=[
            pltpu.VMEM((inds, rows, 128), jnp.int32),
            pltpu.VMEM((inds, rows, 128), jnp.int32),
            pltpu.VMEM((inds, rows, kdim), f32),
            pltpu.VMEM((chunks, 128, 256), f32),
            pltpu.VMEM((chunks, 128, 256), f32),
            pltpu.VMEM((maps, 8, kdim, 128), f32),
            pltpu.VMEM((maps, 8, kdim, 128), f32),
            pltpu.VMEM((maps, kdim, 128), f32),
            pltpu.VMEM((maps, chunks, kdim, 128), f32),
            pltpu.VMEM((maps, 8, kdim, 128), f32),
            pltpu.VMEM((STEPS, 8, 128), f32),
            pltpu.VMEM((STEPS, 8, 8, 128), f32),
            pltpu.VMEM((STEPS, 8, 128), f32),
            pltpu.VMEM((STEPS, chunks, 8, 128), f32),
            pltpu.VMEM((8, kdim, 128), f32),
            pltpu.VMEM((8, kdim, 128), f32),
            pltpu.VMEM((128, kdim), f32),
            pltpu.VMEM((128, kdim), f32),
            pltpu.VMEM((128, kdim), f32),
            dma, dma, dma, dma,
            dma((chunks,)),
            dma((chunks,)),
        ]
        + [dma((maps,))] * 6
        + [dma((STEPS,))] * 4,
        compiler_params=pltpu.CompilerParams(
            collective_id=0, has_side_effects=True, vmem_limit_bytes=40 * 1024 * 1024
        ),
    )(genotypes, observed, ancestry, freqs)


def pick(genotypes, observed, ancestry, freqs):
    inds = lax.axis_size("ind")
    rows, kdim = ancestry.shape
    fits = (
        lax.axis_size("snp") == 2
        and freqs.shape[0] == 128
        and rows == 64
        and kdim == 32
        and inds == 16
    )
    form = fast_device if fits else per_device
    return form(genotypes, observed, ancestry, freqs)


def solution(mesh):
    in_specs = (P("ind", "snp"), P("ind", "snp"), P("ind", None), P(("snp", "ind"), None))
    out_specs = (P("ind", None), P(("snp", "ind"), None))
    return jax.shard_map(pick, mesh=mesh, in_specs=in_specs, out_specs=out_specs, check_vma=False)
```

```python
import functools

import jax
import jax.numpy as jnp
from jax import lax
from jax.experimental import pallas as pl
from jax.experimental.pallas import tpu as pltpu
from jax.sharding import PartitionSpec as P

STEPS = 3


clip_low = 1e-05
high = lax.Precision.HIGHEST
MESH = pl.DeviceIdType.MESH
f32 = jnp.float32
bf16 = jnp.bfloat16


def over_rows(left, right):
    return lax.dot_general(
        left, right, (((0,), (0,)), ((), ())), precision=high, preferred_element_type=jnp.float32
    )


def per_device(genotypes, observed, ancestry, freqs):
    ind_count = lax.axis_size("ind")
    snp_count = lax.axis_size("snp")
    geno = genotypes.astype(jnp.float32)
    seen = observed.astype(jnp.float32)
    hits = seen * geno
    misses = seen * (2.0 - geno)
    own_rows = freqs.shape[0]
    q_zero = ancestry / jnp.sum(ancestry, axis=1, keepdims=True)
    f_zero = lax.all_gather(freqs, "ind", axis=0, tiled=True)
    f_weight = 1.0 / ind_count
    q_weight = 1.0 / snp_count

    def em_map(q_rows, f_state):
        prob = jnp.dot(q_rows, f_state.T, precision=high, preferred_element_type=jnp.float32)
        ratio_a = hits / prob
        ratio_b = misses / (1.0 - prob)
        sum_a = jnp.dot(ratio_a, f_state, precision=high, preferred_element_type=jnp.float32)
        sum_b = jnp.dot(ratio_b, 1.0 - f_state, precision=high, preferred_element_type=jnp.float32)
        c_part = over_rows(ratio_a, q_rows)
        d_part = over_rows(ratio_b, q_rows)
        sum_a, sum_b = lax.psum((sum_a, sum_b), "snp")
        q_next = q_rows * (sum_a + sum_b)
        q_next = q_next / jnp.sum(q_next, axis=1, keepdims=True)
        c_total, d_total = lax.psum((c_part, d_part), "ind")
        f_next = f_state * c_total / (f_state * c_total + (1.0 - f_state) * d_total)
        return (q_next, f_next)

    for step in range(STEPS):
        q_one, f_one = em_map(q_zero, f_zero)
        rq = q_one - q_zero
        rf = f_one - f_zero
        first_local = q_weight * jnp.sum(rq * rq) + f_weight * jnp.sum(rf * rf)
        q_two, f_two = em_map(q_one, f_one)
        vq = q_two - 2.0 * q_one + q_zero
        vf = f_two - 2.0 * f_one + f_zero
        second_local = q_weight * jnp.sum(vq * vq) + f_weight * jnp.sum(vf * vf)
        first, second = lax.psum((first_local, second_local), ("ind", "snp"))
        alpha = -jnp.sqrt(first / (second + 1e-20))
        q_ext = jnp.clip(q_zero - 2.0 * alpha * rq + alpha * alpha * vq, clip_low, 1.0 - clip_low)
        q_zero = q_ext / jnp.sum(q_ext, axis=1, keepdims=True)
        f_zero = jnp.clip(f_zero - 2.0 * alpha * rf + alpha * alpha * vf, clip_low, 1.0 - clip_low)
    f_final = lax.dynamic_slice_in_dim(f_zero, lax.axis_index("ind") * own_rows, own_rows, 0)
    return (q_zero, f_final)


def split3(x):
    one = x.astype(bf16)
    rest = x - one.astype(f32)
    two = rest.astype(bf16)
    three = (rest - two.astype(f32)).astype(bf16)
    return one, two, three


def nn(left, right):
    return jnp.dot(left, right, preferred_element_type=f32)


def nt(left, right):
    return lax.dot_general(left, right, (((1,), (1,)), ((), ())), preferred_element_type=f32)


def total_of(x):
    return jnp.sum(jnp.sum(x, axis=1, keepdims=True), axis=0, keepdims=True)


def kernel(
    inds, geno_ref, obs_ref, anc_ref, freq_ref, q_out, f_out,
    geno_all, obs_all, anc_all, hits, misses, part, rs_in, z_own, z_in, full,
    len_own, len_in, len_sum, len_z,
    q_zero, q_one, f_zero, f_one, flip,
    anc_send, anc_recv, geno_send, obs_send, geno_recv, obs_recv,
    rs_send, rs_recv, z_send, z_recv, ag_send, ag_recv,
    lr_send, lr_recv, lz_send, lz_recv,
):
    me = lax.axis_index("ind")
    core = lax.axis_index("snp")
    other = 1 - core
    rows = geno_ref.shape[0]
    chunks = hits.shape[0]
    kdim = anc_ref.shape[1]
    width = inds.bit_length() - 1
    bits = [lax.rem(lax.div(me, 1 << k), 2) for k in range(width)]

    def flipped(d, low=0):
        j = 0
        for k in range(low, width):
            bit = 1 - bits[k] if (d >> k) & 1 else bits[k]
            j = j + bit * (1 << (k - low))
        return j

    peers = [(d, flipped(d)) for d in range(inds - 1, 0, -1)]

    group = core * 4 + lax.rem(me, 4)
    layer = lax.div(me, 4)
    near = [(flipped(d % 4), other if d >= 4 else core) for d in (7, 3, 6, 5, 2, 1, 4)]
    near = [(j, c, c * 4 + lax.rem(j, 4)) for j, c in near]
    columns = [(flipped(4 * d), core) for d in (3, 2, 1)]

    barrier = pltpu.get_barrier_semaphore()
    for _, j in peers:
        pl.semaphore_signal(barrier, inc=1, device_id=(j, core), device_id_type=MESH)
    for d in range(4):
        pl.semaphore_signal(barrier, inc=1, device_id=(flipped(d), other), device_id_type=MESH)
    pl.semaphore_wait(barrier, inds + 3)

    def remote(src, dst, ssem, rsem, dev):
        return pltpu.make_async_remote_copy(
            src_ref=src, dst_ref=dst, send_sem=ssem, recv_sem=rsem,
            device_id=dev, device_id_type=MESH,
        )

    def send(*args):
        remote(*args).start()

    def arrived(ref, sem):
        pltpu.make_async_copy(ref, ref, sem).wait()

    most = pl.ds(0, inds - 1)
    for _, j in peers:
        send(anc_ref, anc_all.at[me], anc_send, anc_recv, (j, core))
    spread = [(4 * dz + d, flipped(4 * dz + d)) for d in (3, 1, 2, 0) for dz in (3, 2, 1, 0) if dz + d]
    for d, j in spread:
        cols = pl.ds(pl.multiple_of(j * 128, 128), 128)
        send(geno_ref.at[:, cols], geno_all.at[me], geno_send, geno_recv.at[d // 4], (j, core))
        send(obs_ref.at[:, cols], obs_all.at[me], obs_send, obs_recv.at[d // 4], (j, core))
    own = pl.ds(pl.multiple_of(me * 128, 128), 128)
    geno_all[me] = geno_ref[:, own]
    obs_all[me] = obs_ref[:, own]
    anc_all[me] = anc_ref[...]
    f_zero[...] = freq_ref[...]
    arrived(anc_all.at[most], anc_recv)
    for chunk in range(chunks):
        anc = jnp.concatenate([anc_all[4 * chunk + s] for s in range(4)], axis=0).T
        anc = anc / jnp.sum(anc, axis=0, keepdims=True)
        for half in range(2):
            q_zero[2 * chunk + half] = anc[:, 128 * half : 128 * half + 128]

    def lay(cc, chunk):
        count = pl.ds(0, 4 if cc else 3)
        arrived(geno_all.at[count], geno_recv.at[cc])
        arrived(obs_all.at[count], obs_recv.at[cc])
        for half in range(2):
            at = 4 * chunk + 2 * half
            geno = jnp.concatenate([geno_all[at], geno_all[at + 1]], axis=0).astype(f32).T
            seen = jnp.concatenate([obs_all[at], obs_all[at + 1]], axis=0).astype(f32).T
            hits[chunk, :, 128 * half : 128 * half + 128] = seen * geno
            misses[chunk, :, 128 * half : 128 * half + 128] = seen * (2.0 - geno)

    lane = lax.broadcasted_iota(jnp.int32, (8, 128), 1)

    def prepare(f):
        ft = f.T
        f1, f2, f3 = split3(ft)
        lhs = jnp.concatenate([x.astype(f32) for x in (f1, f2, f1, f2, f3, f1, f3, f2)], axis=0).T.astype(bf16)
        g1, g2, g3 = split3(jnp.concatenate([ft, 1.0 - ft], axis=1))
        return lhs, g1, jnp.concatenate([g1, g2], axis=0), jnp.concatenate([g1, g2, g3], axis=0)

    seven = pl.ds(0, 7)
    three = pl.ds(0, chunks - 1)

    def added(ref, at, count):
        total = ref[at, 0]
        for i in range(1, count):
            total = total + ref[at, i]
        return total

    def mixed(k):
        low = lax.rem(lax.div(me, 2), 2)
        return 2 * (other if k & 2 else core) + (1 - low if k & 1 else low)

    def scatter(e, j, c, g):
        send(part.at[e, g], rs_in.at[e, group], rs_send.at[e], rs_recv.at[e], (j, c))

    def em_map(e, q_ref, f, ready, is_first, lengths_of, step):
        lhs, g1, g64, g96 = ready
        kept = []
        for cc in range(chunks):
            chunk = flipped(4 * cc, 2) if is_first else mixed(3 - cc)
            if is_first:
                lay(cc, chunk)
            q1, q2, q3 = split3(jnp.concatenate([q_ref[2 * chunk], q_ref[2 * chunk + 1]], axis=1))
            prob = nn(lhs, jnp.concatenate([q1, q1, q2, q2, q1, q3, q2, q3], axis=0))
            ab = jnp.concatenate([hits[chunk] / prob, misses[chunk] / (1.0 - prob)], axis=0)
            a1, a2, a3 = split3(ab)
            x = nn(g96, a1)
            y = nn(g64, a2)
            sums = x[0:kdim] + (x[kdim : 2 * kdim] + y[0:kdim] + (x[2 * kdim :] + y[kdim:] + nn(g1, a3)))
            for half in range(2):
                part[e, 2 * chunk + half] = sums[:, 128 * half : 128 * half + 128]
            kept.append((a1, a2, a3, q1, q2, q3))
            if not is_first:
                for half in range(2):
                    g = 2 * chunk + half if cc < 3 else group + 1 - 2 * lax.rem(group, 2)
                    if cc < 3 or half == 0:
                        scatter(e, layer * 4 + lax.rem(g, 4), lax.div(g, 4), g)

        if is_first:
            for j, c, g in near:
                scatter(e, j, c, g)
        rs_in[e, group] = part[e, group]

        def products(some):
            u = w = v = 0.0
            for a1, a2, a3, q1, q2, q3 in some:
                u = u + nt(a1, jnp.concatenate([q1, q2, q3], axis=0))
                w = w + nt(a2, jnp.concatenate([q1, q2], axis=0))
                v = v + nt(a3, q1)
            return u, w, v

        early = products(kept[: chunks // 2])
        arrived(rs_in.at[e, seven], rs_recv.at[e])
        z_own[e] = added(rs_in, e, 8)
        for dev in columns:
            send(z_own.at[e], z_in.at[e, layer], z_send.at[e], z_recv.at[e], dev)
        z_in[e, layer] = z_own[e]
        late = products(kept[chunks // 2 :])
        u, w, v = [x + y for x, y in zip(early, late)]
        cd = u[:, 0:kdim] + (u[:, kdim : 2 * kdim] + w[:, 0:kdim] + (u[:, 2 * kdim :] + w[:, kdim:] + v))
        fc = f * cd[0:128]
        f_next = fc / (fc + (1.0 - f) * cd[128:256])
        if lengths_of is not None:
            len_own[step] = lengths_of(f_next)
            for j, c, g in near:
                send(len_own.at[step], len_in.at[step, group], lr_send.at[step], lr_recv.at[step], (j, c))
            len_in[step, group] = len_own[step]
        arrived(z_in.at[e, three], z_recv.at[e])
        grown = q_ref[group] * added(z_in, e, chunks)
        full[e, group] = grown / jnp.sum(grown, axis=0, keepdims=True)
        for j, c, g in near:
            send(full.at[e, group], full.at[e, group], ag_send.at[e], ag_recv.at[e], (j, c))
        later = lengths = None
        if lengths_of is not None:
            arrived(len_in.at[step, seven], lr_recv.at[step])
            len_sum[step] = added(len_in, step, 8)
            for dev in columns:
                send(len_sum.at[step], len_z.at[step, layer], lz_send.at[step], lz_recv.at[step], dev)
            len_z[step, layer] = len_sum[step]
        else:
            later = prepare(f_next)
        arrived(full.at[e, seven], ag_recv.at[e])
        if lengths_of is not None:
            arrived(len_z.at[step, three], lz_recv.at[step])
            lengths = added(len_z, step, chunks)
            arrived(len_in.at[step, seven], lr_send.at[step])
            arrived(len_z.at[step, three], lz_send.at[step])
        arrived(rs_in.at[e, seven], rs_send.at[e])
        arrived(z_in.at[e, three], z_send.at[e])
        arrived(full.at[e, seven], ag_send.at[e])
        return full[e], f_next, later, lengths

    def all_sum(x):
        return total_of(jnp.sum(x, axis=0))

    def one_step(step, is_first):
        f0 = f_zero[...]
        q_first, f_first, ready, _ = em_map(2 * step, q_zero, f0, prepare(f0), is_first, None, step)
        q_one[...] = q_first
        f_one[...] = f_first

        def lengths_of(f_next):
            rf = f_first - f0
            vf = f_next - 2.0 * f_first + f0
            return jnp.where(lane == 0, total_of(rf * rf), jnp.where(lane == 1, total_of(vf * vf), 0.0))

        q_two, f_two, _, lengths = em_map(2 * step + 1, q_one, f_first, ready, False, lengths_of, step)
        q0 = q_zero[...]
        rq = q_one[...] - q0
        vq = q_two - 2.0 * q_one[...] + q0
        rf = f_first - f0
        vf = f_two - 2.0 * f_first + f0
        row = lengths[0:1]
        first = all_sum(rq * rq) + total_of(jnp.where(lane[0:1] == 0, row, 0.0))
        second = all_sum(vq * vq) + total_of(jnp.where(lane[0:1] == 1, row, 0.0))
        alpha = -jnp.sqrt(first / (second + 1e-20))
        q_ext = jnp.clip(q0 - 2.0 * alpha * rq + alpha * alpha * vq, clip_low, 1.0 - clip_low)
        q_zero[...] = q_ext / jnp.sum(q_ext, axis=1, keepdims=True)
        f_zero[...] = jnp.clip(f0 - 2.0 * alpha * rf + alpha * alpha * vf, clip_low, 1.0 - clip_low)

    one_step(0, True)
    arrived(anc_all.at[most], anc_send)
    arrived(geno_all.at[most], geno_send)
    arrived(obs_all.at[most], obs_send)

    def again(step, carry):
        one_step(step, False)
        return carry

    lax.fori_loop(1, STEPS, again, 0)
    f_out[...] = f_zero[...]
    flip[...] = q_zero[lax.div(me, 2)].T
    q_out[...] = flip[pl.ds(pl.multiple_of(lax.rem(me, 2) * rows, rows), rows), :]


def fast_device(genotypes, observed, ancestry, freqs):
    inds = lax.axis_size("ind")
    rows, kdim = ancestry.shape
    people = rows * inds
    chunks = people // 256
    maps = 2 * STEPS
    dma = pltpu.SemaphoreType.DMA
    vmem = pl.BlockSpec(memory_space=pltpu.VMEM)
    return pl.pallas_call(
        functools.partial(kernel, inds),
        out_shape=(
            jax.ShapeDtypeStruct(ancestry.shape, f32),
            jax.ShapeDtypeStruct(freqs.shape, f32),
        ),
        in_specs=[vmem] * 4,
        out_specs=(vmem, vmem),
        scratch_shapes=[
            pltpu.VMEM((inds, rows, 128), jnp.int32),
            pltpu.VMEM((inds, rows, 128), jnp.int32),
            pltpu.VMEM((inds, rows, kdim), f32),
            pltpu.VMEM((chunks, 128, 256), f32),
            pltpu.VMEM((chunks, 128, 256), f32),
            pltpu.VMEM((maps, 8, kdim, 128), f32),
            pltpu.VMEM((maps, 8, kdim, 128), f32),
            pltpu.VMEM((maps, kdim, 128), f32),
            pltpu.VMEM((maps, chunks, kdim, 128), f32),
            pltpu.VMEM((maps, 8, kdim, 128), f32),
            pltpu.VMEM((STEPS, 8, 128), f32),
            pltpu.VMEM((STEPS, 8, 8, 128), f32),
            pltpu.VMEM((STEPS, 8, 128), f32),
            pltpu.VMEM((STEPS, chunks, 8, 128), f32),
            pltpu.VMEM((8, kdim, 128), f32),
            pltpu.VMEM((8, kdim, 128), f32),
            pltpu.VMEM((128, kdim), f32),
            pltpu.VMEM((128, kdim), f32),
            pltpu.VMEM((128, kdim), f32),
            dma, dma, dma, dma,
            dma((chunks,)),
            dma((chunks,)),
        ]
        + [dma((maps,))] * 6
        + [dma((STEPS,))] * 4,
        compiler_params=pltpu.CompilerParams(
            collective_id=0, has_side_effects=True, vmem_limit_bytes=40 * 1024 * 1024
        ),
    )(genotypes, observed, ancestry, freqs)


def pick(genotypes, observed, ancestry, freqs):
    inds = lax.axis_size("ind")
    rows, kdim = ancestry.shape
    fits = (
        lax.axis_size("snp") == 2
        and freqs.shape[0] == 128
        and rows == 64
        and kdim == 32
        and inds == 16
    )
    form = fast_device if fits else per_device
    return form(genotypes, observed, ancestry, freqs)


def solution(mesh):
    in_specs = (P("ind", "snp"), P("ind", "snp"), P("ind", None), P(("snp", "ind"), None))
    out_specs = (P("ind", None), P(("snp", "ind"), None))
    return jax.shard_map(pick, mesh=mesh, in_specs=in_specs, out_specs=out_specs, check_vma=False)
```

```python
import functools

import jax
import jax.numpy as jnp
from jax import lax
from jax.experimental import pallas as pl
from jax.experimental.pallas import tpu as pltpu
from jax.sharding import PartitionSpec as P

STEPS = 3


clip_low = 1e-05
high = lax.Precision.HIGHEST
MESH = pl.DeviceIdType.MESH
f32 = jnp.float32
bf16 = jnp.bfloat16


def over_rows(left, right):
    return lax.dot_general(
        left, right, (((0,), (0,)), ((), ())), precision=high, preferred_element_type=jnp.float32
    )


def per_device(genotypes, observed, ancestry, freqs):
    ind_count = lax.axis_size("ind")
    snp_count = lax.axis_size("snp")
    geno = genotypes.astype(jnp.float32)
    seen = observed.astype(jnp.float32)
    hits = seen * geno
    misses = seen * (2.0 - geno)
    own_rows = freqs.shape[0]
    q_zero = ancestry / jnp.sum(ancestry, axis=1, keepdims=True)
    f_zero = lax.all_gather(freqs, "ind", axis=0, tiled=True)
    f_weight = 1.0 / ind_count
    q_weight = 1.0 / snp_count

    def em_map(q_rows, f_state):
        prob = jnp.dot(q_rows, f_state.T, precision=high, preferred_element_type=jnp.float32)
        ratio_a = hits / prob
        ratio_b = misses / (1.0 - prob)
        sum_a = jnp.dot(ratio_a, f_state, precision=high, preferred_element_type=jnp.float32)
        sum_b = jnp.dot(ratio_b, 1.0 - f_state, precision=high, preferred_element_type=jnp.float32)
        c_part = over_rows(ratio_a, q_rows)
        d_part = over_rows(ratio_b, q_rows)
        sum_a, sum_b = lax.psum((sum_a, sum_b), "snp")
        q_next = q_rows * (sum_a + sum_b)
        q_next = q_next / jnp.sum(q_next, axis=1, keepdims=True)
        c_total, d_total = lax.psum((c_part, d_part), "ind")
        f_next = f_state * c_total / (f_state * c_total + (1.0 - f_state) * d_total)
        return (q_next, f_next)

    for step in range(STEPS):
        q_one, f_one = em_map(q_zero, f_zero)
        rq = q_one - q_zero
        rf = f_one - f_zero
        first_local = q_weight * jnp.sum(rq * rq) + f_weight * jnp.sum(rf * rf)
        q_two, f_two = em_map(q_one, f_one)
        vq = q_two - 2.0 * q_one + q_zero
        vf = f_two - 2.0 * f_one + f_zero
        second_local = q_weight * jnp.sum(vq * vq) + f_weight * jnp.sum(vf * vf)
        first, second = lax.psum((first_local, second_local), ("ind", "snp"))
        alpha = -jnp.sqrt(first / (second + 1e-20))
        q_ext = jnp.clip(q_zero - 2.0 * alpha * rq + alpha * alpha * vq, clip_low, 1.0 - clip_low)
        q_zero = q_ext / jnp.sum(q_ext, axis=1, keepdims=True)
        f_zero = jnp.clip(f_zero - 2.0 * alpha * rf + alpha * alpha * vf, clip_low, 1.0 - clip_low)
    f_final = lax.dynamic_slice_in_dim(f_zero, lax.axis_index("ind") * own_rows, own_rows, 0)
    return (q_zero, f_final)


def split3(x):
    one = x.astype(bf16)
    rest = x - one.astype(f32)
    two = rest.astype(bf16)
    three = (rest - two.astype(f32)).astype(bf16)
    return one, two, three


def nn(left, right):
    return jnp.dot(left, right, preferred_element_type=f32)


def nt(left, right):
    return lax.dot_general(left, right, (((1,), (1,)), ((), ())), preferred_element_type=f32)


def total_of(x):
    return jnp.sum(jnp.sum(x, axis=1, keepdims=True), axis=0, keepdims=True)


def kernel(
    inds, geno_ref, obs_ref, anc_ref, freq_ref, q_out, f_out,
    geno_all, obs_all, anc_all, hits, misses, part, rs_in, z_own, z_in, full,
    len_own, len_in, len_sum, len_z,
    q_zero, q_one, f_zero, f_one, flip,
    anc_send, anc_recv, geno_send, obs_send, geno_recv, obs_recv,
    rs_send, rs_recv, z_send, z_recv, ag_send, ag_recv,
    lr_send, lr_recv, lz_send, lz_recv, own_sem,
):
    me = lax.axis_index("ind")
    core = lax.axis_index("snp")
    other = 1 - core
    rows = geno_ref.shape[0]
    chunks = hits.shape[0]
    kdim = anc_ref.shape[1]
    width = inds.bit_length() - 1
    bits = [lax.rem(lax.div(me, 1 << k), 2) for k in range(width)]

    def flipped(d, low=0):
        j = 0
        for k in range(low, width):
            bit = 1 - bits[k] if (d >> k) & 1 else bits[k]
            j = j + bit * (1 << (k - low))
        return j

    peers = [(d, flipped(d)) for d in range(inds - 1, 0, -1)]

    group = core * 4 + lax.rem(me, 4)
    layer = lax.div(me, 4)
    near = [(flipped(d % 4), other if d >= 4 else core) for d in (7, 3, 6, 5, 2, 1, 4)]
    near = [(j, c, c * 4 + lax.rem(j, 4)) for j, c in near]
    columns = [(flipped(4 * d), core) for d in (3, 2, 1)]

    barrier = pltpu.get_barrier_semaphore()
    for _, j in peers:
        pl.semaphore_signal(barrier, inc=1, device_id=(j, core), device_id_type=MESH)
    for d in range(4):
        pl.semaphore_signal(barrier, inc=1, device_id=(flipped(d), other), device_id_type=MESH)
    pl.semaphore_wait(barrier, inds + 3)

    def remote(src, dst, ssem, rsem, dev):
        return pltpu.make_async_remote_copy(
            src_ref=src, dst_ref=dst, send_sem=ssem, recv_sem=rsem,
            device_id=dev, device_id_type=MESH,
        )

    def send(*args):
        remote(*args).start()

    def arrived(ref, sem):
        pltpu.make_async_copy(ref, ref, sem).wait()

    most = pl.ds(0, inds - 1)
    for _, j in peers:
        send(anc_ref, anc_all.at[me], anc_send, anc_recv, (j, core))
    for d, j in peers:
        cols = pl.ds(pl.multiple_of(j * 128, 128), 128)
        send(geno_ref.at[:, cols], geno_all.at[me], geno_send, geno_recv.at[d // 4], (j, core))
        send(obs_ref.at[:, cols], obs_all.at[me], obs_send, obs_recv.at[d // 4], (j, core))
    own = pl.ds(pl.multiple_of(me * 128, 128), 128)
    geno_own = pltpu.make_async_copy(geno_ref.at[:, own], geno_all.at[me], own_sem.at[0])
    obs_own = pltpu.make_async_copy(obs_ref.at[:, own], obs_all.at[me], own_sem.at[1])
    geno_own.start()
    obs_own.start()
    anc_all[me] = anc_ref[...]
    f_zero[...] = freq_ref[...]
    geno_own.wait()
    obs_own.wait()
    arrived(anc_all.at[most], anc_recv)
    for chunk in range(chunks):
        anc = jnp.concatenate([anc_all[4 * chunk + s] for s in range(4)], axis=0).T
        anc = anc / jnp.sum(anc, axis=0, keepdims=True)
        for half in range(2):
            q_zero[2 * chunk + half] = anc[:, 128 * half : 128 * half + 128]

    def lay(cc, chunk):
        count = pl.ds(0, 4 if cc else 3)
        arrived(geno_all.at[count], geno_recv.at[cc])
        arrived(obs_all.at[count], obs_recv.at[cc])
        for half in range(2):
            at = 4 * chunk + 2 * half
            geno = jnp.concatenate([geno_all[at], geno_all[at + 1]], axis=0).astype(f32).T
            seen = jnp.concatenate([obs_all[at], obs_all[at + 1]], axis=0).astype(f32).T
            hits[chunk, :, 128 * half : 128 * half + 128] = seen * geno
            misses[chunk, :, 128 * half : 128 * half + 128] = seen * (2.0 - geno)

    lane = lax.broadcasted_iota(jnp.int32, (8, 128), 1)

    def prepare(f):
        ft = f.T
        f1, f2, f3 = split3(ft)
        lhs = jnp.concatenate([x.astype(f32) for x in (f1, f2, f1, f2, f3, f1, f3, f2)], axis=0).T.astype(bf16)
        g1, g2, g3 = split3(jnp.concatenate([ft, 1.0 - ft], axis=1))
        return lhs, g1, jnp.concatenate([g1, g2], axis=0), jnp.concatenate([g1, g2, g3], axis=0)

    seven = pl.ds(0, 7)
    three = pl.ds(0, chunks - 1)

    def added(ref, at, count):
        total = ref[at, 0]
        for i in range(1, count):
            total = total + ref[at, i]
        return total

    def em_map(e, q_ref, f, ready, is_first, lengths_of, step):
        lhs, g1, g64, g96 = ready
        kept = []
        for cc in range(chunks):
            chunk = flipped(4 * cc, 2) if is_first else cc
            if is_first:
                lay(cc, chunk)
            q1, q2, q3 = split3(jnp.concatenate([q_ref[2 * chunk], q_ref[2 * chunk + 1]], axis=1))
            prob = nn(lhs, jnp.concatenate([q1, q1, q2, q2, q1, q3, q2, q3], axis=0))
            ab = jnp.concatenate([hits[chunk] / prob, misses[chunk] / (1.0 - prob)], axis=0)
            a1, a2, a3 = split3(ab)
            x = nn(g96, a1)
            y = nn(g64, a2)
            sums = x[0:kdim] + (x[kdim : 2 * kdim] + y[0:kdim] + (x[2 * kdim :] + y[kdim:] + nn(g1, a3)))
            for half in range(2):
                part[e, 2 * chunk + half] = sums[:, 128 * half : 128 * half + 128]
            kept.append((a1, a2, a3, q1, q2, q3))

        for j, c, g in near:
            send(part.at[e, g], rs_in.at[e, group], rs_send.at[e], rs_recv.at[e], (j, c))
        rs_in[e, group] = part[e, group]

        def products(some):
            u = w = v = 0.0
            for a1, a2, a3, q1, q2, q3 in some:
                u = u + nt(a1, jnp.concatenate([q1, q2, q3], axis=0))
                w = w + nt(a2, jnp.concatenate([q1, q2], axis=0))
                v = v + nt(a3, q1)
            return u, w, v

        early = products(kept[: chunks // 2])
        arrived(rs_in.at[e, seven], rs_recv.at[e])
        z_own[e] = added(rs_in, e, 8)
        for dev in columns:
            send(z_own.at[e], z_in.at[e, layer], z_send.at[e], z_recv.at[e], dev)
        z_in[e, layer] = z_own[e]
        late = products(kept[chunks // 2 :])
        u, w, v = [x + y for x, y in zip(early, late)]
        cd = u[:, 0:kdim] + (u[:, kdim : 2 * kdim] + w[:, 0:kdim] + (u[:, 2 * kdim :] + w[:, kdim:] + v))
        fc = f * cd[0:128]
        f_next = fc / (fc + (1.0 - f) * cd[128:256])
        if lengths_of is not None:
            len_own[step] = lengths_of(f_next)
            for j, c, g in near:
                send(len_own.at[step], len_in.at[step, group], lr_send.at[step], lr_recv.at[step], (j, c))
            len_in[step, group] = len_own[step]
        arrived(z_in.at[e, three], z_recv.at[e])
        grown = q_ref[group] * added(z_in, e, chunks)
        full[e, group] = grown / jnp.sum(grown, axis=0, keepdims=True)
        for j, c, g in near:
            send(full.at[e, group], full.at[e, group], ag_send.at[e], ag_recv.at[e], (j, c))
        later = lengths = None
        if lengths_of is not None:
            arrived(len_in.at[step, seven], lr_recv.at[step])
            len_sum[step] = added(len_in, step, 8)
            for dev in columns:
                send(len_sum.at[step], len_z.at[step, layer], lz_send.at[step], lz_recv.at[step], dev)
            len_z[step, layer] = len_sum[step]
        else:
            later = prepare(f_next)
        arrived(full.at[e, seven], ag_recv.at[e])
        if lengths_of is not None:
            arrived(len_z.at[step, three], lz_recv.at[step])
            lengths = added(len_z, step, chunks)
            arrived(len_in.at[step, seven], lr_send.at[step])
            arrived(len_z.at[step, three], lz_send.at[step])
        arrived(rs_in.at[e, seven], rs_send.at[e])
        arrived(z_in.at[e, three], z_send.at[e])
        arrived(full.at[e, seven], ag_send.at[e])
        return full[e], f_next, later, lengths

    def all_sum(x):
        return total_of(jnp.sum(x, axis=0))

    def one_step(step, is_first):
        f0 = f_zero[...]
        q_first, f_first, ready, _ = em_map(2 * step, q_zero, f0, prepare(f0), is_first, None, step)
        q_one[...] = q_first
        f_one[...] = f_first

        def lengths_of(f_next):
            rf = f_first - f0
            vf = f_next - 2.0 * f_first + f0
            return jnp.where(lane == 0, total_of(rf * rf), jnp.where(lane == 1, total_of(vf * vf), 0.0))

        q_two, f_two, _, lengths = em_map(2 * step + 1, q_one, f_first, ready, False, lengths_of, step)
        q0 = q_zero[...]
        rq = q_one[...] - q0
        vq = q_two - 2.0 * q_one[...] + q0
        rf = f_first - f0
        vf = f_two - 2.0 * f_first + f0
        row = lengths[0:1]
        first = all_sum(rq * rq) + total_of(jnp.where(lane[0:1] == 0, row, 0.0))
        second = all_sum(vq * vq) + total_of(jnp.where(lane[0:1] == 1, row, 0.0))
        alpha = -jnp.sqrt(first / (second + 1e-20))
        q_ext = jnp.clip(q0 - 2.0 * alpha * rq + alpha * alpha * vq, clip_low, 1.0 - clip_low)
        q_zero[...] = q_ext / jnp.sum(q_ext, axis=1, keepdims=True)
        f_zero[...] = jnp.clip(f0 - 2.0 * alpha * rf + alpha * alpha * vf, clip_low, 1.0 - clip_low)

    one_step(0, True)
    arrived(anc_all.at[most], anc_send)
    arrived(geno_all.at[most], geno_send)
    arrived(obs_all.at[most], obs_send)

    def again(step, carry):
        one_step(step, False)
        return carry

    lax.fori_loop(1, STEPS, again, 0)
    f_out[...] = f_zero[...]
    flip[...] = q_zero[lax.div(me, 2)].T
    q_out[...] = flip[pl.ds(pl.multiple_of(lax.rem(me, 2) * rows, rows), rows), :]


def fast_device(genotypes, observed, ancestry, freqs):
    inds = lax.axis_size("ind")
    rows, kdim = ancestry.shape
    people = rows * inds
    chunks = people // 256
    maps = 2 * STEPS
    dma = pltpu.SemaphoreType.DMA
    vmem = pl.BlockSpec(memory_space=pltpu.VMEM)
    return pl.pallas_call(
        functools.partial(kernel, inds),
        out_shape=(
            jax.ShapeDtypeStruct(ancestry.shape, f32),
            jax.ShapeDtypeStruct(freqs.shape, f32),
        ),
        in_specs=[pl.BlockSpec(memory_space=pl.ANY)] * 2 + [vmem] * 2,
        out_specs=(vmem, vmem),
        scratch_shapes=[
            pltpu.VMEM((inds, rows, 128), jnp.int32),
            pltpu.VMEM((inds, rows, 128), jnp.int32),
            pltpu.VMEM((inds, rows, kdim), f32),
            pltpu.VMEM((chunks, 128, 256), f32),
            pltpu.VMEM((chunks, 128, 256), f32),
            pltpu.VMEM((maps, 8, kdim, 128), f32),
            pltpu.VMEM((maps, 8, kdim, 128), f32),
            pltpu.VMEM((maps, kdim, 128), f32),
            pltpu.VMEM((maps, chunks, kdim, 128), f32),
            pltpu.VMEM((maps, 8, kdim, 128), f32),
            pltpu.VMEM((STEPS, 8, 128), f32),
            pltpu.VMEM((STEPS, 8, 8, 128), f32),
            pltpu.VMEM((STEPS, 8, 128), f32),
            pltpu.VMEM((STEPS, chunks, 8, 128), f32),
            pltpu.VMEM((8, kdim, 128), f32),
            pltpu.VMEM((8, kdim, 128), f32),
            pltpu.VMEM((128, kdim), f32),
            pltpu.VMEM((128, kdim), f32),
            pltpu.VMEM((128, kdim), f32),
            dma, dma, dma, dma,
            dma((chunks,)),
            dma((chunks,)),
        ]
        + [dma((maps,))] * 6
        + [dma((STEPS,))] * 4
        + [dma((2,))],
        compiler_params=pltpu.CompilerParams(
            collective_id=0, has_side_effects=True, vmem_limit_bytes=40 * 1024 * 1024
        ),
    )(genotypes, observed, ancestry, freqs)


def pick(genotypes, observed, ancestry, freqs):
    inds = lax.axis_size("ind")
    rows, kdim = ancestry.shape
    fits = (
        lax.axis_size("snp") == 2
        and freqs.shape[0] == 128
        and rows == 64
        and kdim == 32
        and inds == 16
    )
    form = fast_device if fits else per_device
    return form(genotypes, observed, ancestry, freqs)


def solution(mesh):
    in_specs = (P("ind", "snp"), P("ind", "snp"), P("ind", None), P(("snp", "ind"), None))
    out_specs = (P("ind", None), P(("snp", "ind"), None))
    return jax.shard_map(pick, mesh=mesh, in_specs=in_specs, out_specs=out_specs, check_vma=False)
```

```python
import functools

import jax
import jax.numpy as jnp
from jax import lax
from jax.experimental import pallas as pl
from jax.experimental.pallas import tpu as pltpu
from jax.sharding import PartitionSpec as P

STEPS = 3


clip_low = 1e-05
high = lax.Precision.HIGHEST
MESH = pl.DeviceIdType.MESH
f32 = jnp.float32
bf16 = jnp.bfloat16


def over_rows(left, right):
    return lax.dot_general(
        left, right, (((0,), (0,)), ((), ())), precision=high, preferred_element_type=jnp.float32
    )


def per_device(genotypes, observed, ancestry, freqs):
    ind_count = lax.axis_size("ind")
    snp_count = lax.axis_size("snp")
    geno = genotypes.astype(jnp.float32)
    seen = observed.astype(jnp.float32)
    hits = seen * geno
    misses = seen * (2.0 - geno)
    own_rows = freqs.shape[0]
    q_zero = ancestry / jnp.sum(ancestry, axis=1, keepdims=True)
    f_zero = lax.all_gather(freqs, "ind", axis=0, tiled=True)
    f_weight = 1.0 / ind_count
    q_weight = 1.0 / snp_count

    def em_map(q_rows, f_state):
        prob = jnp.dot(q_rows, f_state.T, precision=high, preferred_element_type=jnp.float32)
        ratio_a = hits / prob
        ratio_b = misses / (1.0 - prob)
        sum_a = jnp.dot(ratio_a, f_state, precision=high, preferred_element_type=jnp.float32)
        sum_b = jnp.dot(ratio_b, 1.0 - f_state, precision=high, preferred_element_type=jnp.float32)
        c_part = over_rows(ratio_a, q_rows)
        d_part = over_rows(ratio_b, q_rows)
        sum_a, sum_b = lax.psum((sum_a, sum_b), "snp")
        q_next = q_rows * (sum_a + sum_b)
        q_next = q_next / jnp.sum(q_next, axis=1, keepdims=True)
        c_total, d_total = lax.psum((c_part, d_part), "ind")
        f_next = f_state * c_total / (f_state * c_total + (1.0 - f_state) * d_total)
        return (q_next, f_next)

    for step in range(STEPS):
        q_one, f_one = em_map(q_zero, f_zero)
        rq = q_one - q_zero
        rf = f_one - f_zero
        first_local = q_weight * jnp.sum(rq * rq) + f_weight * jnp.sum(rf * rf)
        q_two, f_two = em_map(q_one, f_one)
        vq = q_two - 2.0 * q_one + q_zero
        vf = f_two - 2.0 * f_one + f_zero
        second_local = q_weight * jnp.sum(vq * vq) + f_weight * jnp.sum(vf * vf)
        first, second = lax.psum((first_local, second_local), ("ind", "snp"))
        alpha = -jnp.sqrt(first / (second + 1e-20))
        q_ext = jnp.clip(q_zero - 2.0 * alpha * rq + alpha * alpha * vq, clip_low, 1.0 - clip_low)
        q_zero = q_ext / jnp.sum(q_ext, axis=1, keepdims=True)
        f_zero = jnp.clip(f_zero - 2.0 * alpha * rf + alpha * alpha * vf, clip_low, 1.0 - clip_low)
    f_final = lax.dynamic_slice_in_dim(f_zero, lax.axis_index("ind") * own_rows, own_rows, 0)
    return (q_zero, f_final)


def split3(x):
    one = x.astype(bf16)
    rest = x - one.astype(f32)
    two = rest.astype(bf16)
    three = (rest - two.astype(f32)).astype(bf16)
    return one, two, three


def nn(left, right):
    return jnp.dot(left, right, preferred_element_type=f32)


def nt(left, right):
    return lax.dot_general(left, right, (((1,), (1,)), ((), ())), preferred_element_type=f32)


def total_of(x):
    return jnp.sum(jnp.sum(x, axis=1, keepdims=True), axis=0, keepdims=True)


def kernel(
    inds, geno_ref, obs_ref, anc_ref, freq_ref, q_out, f_out,
    geno_all, obs_all, anc_all, hits, misses, part, rs_in, z_own, z_in, full,
    len_own, len_in, len_sum, len_z,
    q_zero, q_one, f_zero, f_one, flip,
    anc_send, anc_recv, geno_send, obs_send, geno_recv, obs_recv,
    rs_send, rs_recv, z_send, z_recv, ag_send, ag_recv,
    lr_send, lr_recv, lz_send, lz_recv, own_sem,
):
    me = lax.axis_index("ind")
    core = lax.axis_index("snp")
    other = 1 - core
    rows = geno_ref.shape[0]
    chunks = hits.shape[0]
    kdim = anc_ref.shape[1]
    width = inds.bit_length() - 1
    bits = [lax.rem(lax.div(me, 1 << k), 2) for k in range(width)]

    def flipped(d, low=0):
        j = 0
        for k in range(low, width):
            bit = 1 - bits[k] if (d >> k) & 1 else bits[k]
            j = j + bit * (1 << (k - low))
        return j

    peers = [(d, flipped(d)) for d in range(inds - 1, 0, -1)]

    group = core * 4 + lax.rem(me, 4)
    layer = lax.div(me, 4)
    near = [(flipped(d % 4), other if d >= 4 else core) for d in (7, 3, 6, 5, 2, 1, 4)]
    near = [(j, c, c * 4 + lax.rem(j, 4)) for j, c in near]
    columns = [(flipped(4 * d), core) for d in (3, 2, 1)]

    barrier = pltpu.get_barrier_semaphore()
    for _, j in peers:
        pl.semaphore_signal(barrier, inc=1, device_id=(j, core), device_id_type=MESH)
    for d in range(4):
        pl.semaphore_signal(barrier, inc=1, device_id=(flipped(d), other), device_id_type=MESH)
    pl.semaphore_wait(barrier, inds + 3)

    def remote(src, dst, ssem, rsem, dev):
        return pltpu.make_async_remote_copy(
            src_ref=src, dst_ref=dst, send_sem=ssem, recv_sem=rsem,
            device_id=dev, device_id_type=MESH,
        )

    def send(*args):
        remote(*args).start()

    def arrived(ref, sem):
        pltpu.make_async_copy(ref, ref, sem).wait()

    most = pl.ds(0, inds - 1)
    for _, j in peers:
        send(anc_ref, anc_all.at[me], anc_send, anc_recv, (j, core))
    for d, j in peers:
        cols = pl.ds(pl.multiple_of(j * 128, 128), 128)
        send(geno_ref.at[:, cols], geno_all.at[me], geno_send, geno_recv.at[d // 4], (j, core))
        send(obs_ref.at[:, cols], obs_all.at[me], obs_send, obs_recv.at[d // 4], (j, core))
    own = pl.ds(pl.multiple_of(me * 128, 128), 128)
    geno_own = pltpu.make_async_copy(geno_ref.at[:, own], geno_all.at[me], own_sem.at[0])
    obs_own = pltpu.make_async_copy(obs_ref.at[:, own], obs_all.at[me], own_sem.at[1])
    geno_own.start()
    obs_own.start()
    anc_all[me] = anc_ref[...]
    f_zero[...] = freq_ref[...]
    geno_own.wait()
    obs_own.wait()
    arrived(anc_all.at[most], anc_recv)
    for chunk in range(chunks):
        anc = jnp.concatenate([anc_all[4 * chunk + s] for s in range(4)], axis=0).T
        anc = anc / jnp.sum(anc, axis=0, keepdims=True)
        for half in range(2):
            q_zero[2 * chunk + half] = anc[:, 128 * half : 128 * half + 128]

    def lay(cc, chunk):
        count = pl.ds(0, 4 if cc else 3)
        arrived(geno_all.at[count], geno_recv.at[cc])
        arrived(obs_all.at[count], obs_recv.at[cc])
        for half in range(2):
            at = 4 * chunk + 2 * half
            geno = jnp.concatenate([geno_all[at], geno_all[at + 1]], axis=0).astype(f32).T
            seen = jnp.concatenate([obs_all[at], obs_all[at + 1]], axis=0).astype(f32).T
            hits[chunk, :, 128 * half : 128 * half + 128] = seen * geno
            misses[chunk, :, 128 * half : 128 * half + 128] = seen * (2.0 - geno)

    lane = lax.broadcasted_iota(jnp.int32, (8, 128), 1)

    def prepare(f):
        ft = f.T
        f1, f2, f3 = split3(ft)
        lhs = jnp.concatenate([x.astype(f32) for x in (f1, f2, f1, f2, f3, f1, f3, f2)], axis=0).T.astype(bf16)
        g1, g2, g3 = split3(jnp.concatenate([ft, 1.0 - ft], axis=1))
        return lhs, g1, jnp.concatenate([g1, g2], axis=0), jnp.concatenate([g1, g2, g3], axis=0)

    seven = pl.ds(0, 7)
    three = pl.ds(0, chunks - 1)

    def added(ref, at, count):
        total = ref[at, 0]
        for i in range(1, count):
            total = total + ref[at, i]
        return total

    def em_map(e, q_ref, f, ready, is_first, lengths_of, step):
        lhs, g1, g64, g96 = ready
        kept = []
        for cc in range(chunks):
            chunk = flipped(4 * cc, 2) if is_first else cc
            if is_first:
                lay(cc, chunk)
            q1, q2, q3 = split3(jnp.concatenate([q_ref[2 * chunk], q_ref[2 * chunk + 1]], axis=1))
            prob = nn(lhs, jnp.concatenate([q1, q1, q2, q2, q1, q3, q2, q3], axis=0))
            rest = 1.0 - prob
            inverse = 1.0 / (prob * rest)
            ab = jnp.concatenate([hits[chunk] * (rest * inverse), misses[chunk] * (prob * inverse)], axis=0)
            a1, a2, a3 = split3(ab)
            x = nn(g96, a1)
            y = nn(g64, a2)
            sums = x[0:kdim] + (x[kdim : 2 * kdim] + y[0:kdim] + (x[2 * kdim :] + y[kdim:] + nn(g1, a3)))
            for half in range(2):
                part[e, 2 * chunk + half] = sums[:, 128 * half : 128 * half + 128]
            kept.append((a1, a2, a3, q1, q2, q3))

        for j, c, g in near:
            send(part.at[e, g], rs_in.at[e, group], rs_send.at[e], rs_recv.at[e], (j, c))
        rs_in[e, group] = part[e, group]

        def products(some):
            u = w = v = 0.0
            for a1, a2, a3, q1, q2, q3 in some:
                u = u + nt(a1, jnp.concatenate([q1, q2, q3], axis=0))
                w = w + nt(a2, jnp.concatenate([q1, q2], axis=0))
                v = v + nt(a3, q1)
            return u, w, v

        early = products(kept[: chunks // 2])
        arrived(rs_in.at[e, seven], rs_recv.at[e])
        z_own[e] = added(rs_in, e, 8)
        for dev in columns:
            send(z_own.at[e], z_in.at[e, layer], z_send.at[e], z_recv.at[e], dev)
        z_in[e, layer] = z_own[e]
        late = products(kept[chunks // 2 :])
        u, w, v = [x + y for x, y in zip(early, late)]
        cd = u[:, 0:kdim] + (u[:, kdim : 2 * kdim] + w[:, 0:kdim] + (u[:, 2 * kdim :] + w[:, kdim:] + v))
        fc = f * cd[0:128]
        f_next = fc / (fc + (1.0 - f) * cd[128:256])
        if lengths_of is not None:
            len_own[step] = lengths_of(f_next)
            for j, c, g in near:
                send(len_own.at[step], len_in.at[step, group], lr_send.at[step], lr_recv.at[step], (j, c))
            len_in[step, group] = len_own[step]
        arrived(z_in.at[e, three], z_recv.at[e])
        grown = q_ref[group] * added(z_in, e, chunks)
        full[e, group] = grown / jnp.sum(grown, axis=0, keepdims=True)
        for j, c, g in near:
            send(full.at[e, group], full.at[e, group], ag_send.at[e], ag_recv.at[e], (j, c))
        later = lengths = None
        if lengths_of is not None:
            arrived(len_in.at[step, seven], lr_recv.at[step])
            len_sum[step] = added(len_in, step, 8)
            for dev in columns:
                send(len_sum.at[step], len_z.at[step, layer], lz_send.at[step], lz_recv.at[step], dev)
            len_z[step, layer] = len_sum[step]
        else:
            later = prepare(f_next)
        arrived(full.at[e, seven], ag_recv.at[e])
        if lengths_of is not None:
            arrived(len_z.at[step, three], lz_recv.at[step])
            lengths = added(len_z, step, chunks)
            arrived(len_in.at[step, seven], lr_send.at[step])
            arrived(len_z.at[step, three], lz_send.at[step])
        arrived(rs_in.at[e, seven], rs_send.at[e])
        arrived(z_in.at[e, three], z_send.at[e])
        arrived(full.at[e, seven], ag_send.at[e])
        return full[e], f_next, later, lengths

    def all_sum(x):
        return total_of(jnp.sum(x, axis=0))

    def one_step(step, is_first):
        f0 = f_zero[...]
        q_first, f_first, ready, _ = em_map(2 * step, q_zero, f0, prepare(f0), is_first, None, step)
        q_one[...] = q_first
        f_one[...] = f_first

        def lengths_of(f_next):
            rf = f_first - f0
            vf = f_next - 2.0 * f_first + f0
            return jnp.where(lane == 0, total_of(rf * rf), jnp.where(lane == 1, total_of(vf * vf), 0.0))

        q_two, f_two, _, lengths = em_map(2 * step + 1, q_one, f_first, ready, False, lengths_of, step)
        q0 = q_zero[...]
        rq = q_one[...] - q0
        vq = q_two - 2.0 * q_one[...] + q0
        rf = f_first - f0
        vf = f_two - 2.0 * f_first + f0
        row = lengths[0:1]
        first = all_sum(rq * rq) + total_of(jnp.where(lane[0:1] == 0, row, 0.0))
        second = all_sum(vq * vq) + total_of(jnp.where(lane[0:1] == 1, row, 0.0))
        alpha = -jnp.sqrt(first / (second + 1e-20))
        q_ext = jnp.clip(q0 - 2.0 * alpha * rq + alpha * alpha * vq, clip_low, 1.0 - clip_low)
        q_zero[...] = q_ext / jnp.sum(q_ext, axis=1, keepdims=True)
        f_zero[...] = jnp.clip(f0 - 2.0 * alpha * rf + alpha * alpha * vf, clip_low, 1.0 - clip_low)

    one_step(0, True)
    arrived(anc_all.at[most], anc_send)
    arrived(geno_all.at[most], geno_send)
    arrived(obs_all.at[most], obs_send)

    def again(step, carry):
        one_step(step, False)
        return carry

    lax.fori_loop(1, STEPS, again, 0)
    f_out[...] = f_zero[...]
    flip[...] = q_zero[lax.div(me, 2)].T
    q_out[...] = flip[pl.ds(pl.multiple_of(lax.rem(me, 2) * rows, rows), rows), :]


def fast_device(genotypes, observed, ancestry, freqs):
    inds = lax.axis_size("ind")
    rows, kdim = ancestry.shape
    people = rows * inds
    chunks = people // 256
    maps = 2 * STEPS
    dma = pltpu.SemaphoreType.DMA
    vmem = pl.BlockSpec(memory_space=pltpu.VMEM)
    return pl.pallas_call(
        functools.partial(kernel, inds),
        out_shape=(
            jax.ShapeDtypeStruct(ancestry.shape, f32),
            jax.ShapeDtypeStruct(freqs.shape, f32),
        ),
        in_specs=[pl.BlockSpec(memory_space=pl.ANY)] * 2 + [vmem] * 2,
        out_specs=(vmem, vmem),
        scratch_shapes=[
            pltpu.VMEM((inds, rows, 128), jnp.int32),
            pltpu.VMEM((inds, rows, 128), jnp.int32),
            pltpu.VMEM((inds, rows, kdim), f32),
            pltpu.VMEM((chunks, 128, 256), f32),
            pltpu.VMEM((chunks, 128, 256), f32),
            pltpu.VMEM((maps, 8, kdim, 128), f32),
            pltpu.VMEM((maps, 8, kdim, 128), f32),
            pltpu.VMEM((maps, kdim, 128), f32),
            pltpu.VMEM((maps, chunks, kdim, 128), f32),
            pltpu.VMEM((maps, 8, kdim, 128), f32),
            pltpu.VMEM((STEPS, 8, 128), f32),
            pltpu.VMEM((STEPS, 8, 8, 128), f32),
            pltpu.VMEM((STEPS, 8, 128), f32),
            pltpu.VMEM((STEPS, chunks, 8, 128), f32),
            pltpu.VMEM((8, kdim, 128), f32),
            pltpu.VMEM((8, kdim, 128), f32),
            pltpu.VMEM((128, kdim), f32),
            pltpu.VMEM((128, kdim), f32),
            pltpu.VMEM((128, kdim), f32),
            dma, dma, dma, dma,
            dma((chunks,)),
            dma((chunks,)),
        ]
        + [dma((maps,))] * 6
        + [dma((STEPS,))] * 4
        + [dma((2,))],
        compiler_params=pltpu.CompilerParams(
            collective_id=0, has_side_effects=True, vmem_limit_bytes=40 * 1024 * 1024
        ),
    )(genotypes, observed, ancestry, freqs)


def pick(genotypes, observed, ancestry, freqs):
    inds = lax.axis_size("ind")
    rows, kdim = ancestry.shape
    fits = (
        lax.axis_size("snp") == 2
        and freqs.shape[0] == 128
        and rows == 64
        and kdim == 32
        and inds == 16
    )
    form = fast_device if fits else per_device
    return form(genotypes, observed, ancestry, freqs)


def solution(mesh):
    in_specs = (P("ind", "snp"), P("ind", "snp"), P("ind", None), P(("snp", "ind"), None))
    out_specs = (P("ind", None), P(("snp", "ind"), None))
    return jax.shard_map(pick, mesh=mesh, in_specs=in_specs, out_specs=out_specs, check_vma=False)
```
